256 devices in a mesh: dp: 8 (over y, core), expert: 32 (over x, z).
Axes of the slice: x: 4, y: 4, z: 8, core: 2. Of those that a mesh axis runs over, the one named last changes fastest.
Arguments:
- tokens: bfloat16 [32768, 2048], P(('dp', 'expert')), may hold values from -6 to 6
- cotangent: bfloat16 [32768, 2048], P(('dp', 'expert')), may hold values from -6 to 6
- routed_slots: int32 [32768, 2], P(('dp', 'expert')), may hold values from 0 to 31, all different within a row; in each aligned block of 128 rows (0 to 127, 128 to 255, ...) at most 10 rows name the same one
- route_probs: bfloat16 [32768, 2], P(('dp', 'expert')), may hold values from 0.049804688 to 1
- placement: int32 [32], replicated, may hold values from 0 to 15, as said below
- w_gate: bfloat16 [16, 768, 2048], P(None, 'expert'), may hold values from -0.125 to 0.125
- w_up: bfloat16 [16, 768, 2048], P(None, 'expert'), may hold values from -0.125 to 0.125
- w_down: bfloat16 [16, 768, 2048], P(None, 'expert'), may hold values from -0.21875 to 0.21875
Outputs:
- token_grad: bfloat16 [32768, 2048], P(('dp', 'expert'))
- prob_grad: bfloat16 [32768, 2], P(('dp', 'expert'))
- grad_gate: bfloat16 [16, 768, 2048], P(None, 'expert', 'dp')
- grad_up: bfloat16 [16, 768, 2048], P(None, 'expert', 'dp')
- grad_down: bfloat16 [16, 768, 2048], P(None, 'expert', 'dp')
The draws below stay inside these ranges and needn't reach their ends.
Inputs may be any that keep to these rules, and one draw needn't show every extreme that they name: `routed_slots`: each token names 2 different slots. Of the 128 rows of one device, at most 10 name any one slot. `placement`: every expert is hosted by one slot or more.
All inputs are finite; a program needn't handle non-finite values.
Results may differ from the reference program's by a relative error of at most 0.018.
Values may be sent and summed in bfloat16 or wider, within the bound.
No kernel may reach another device: no remote copies, remote signals or barrier semaphores. Data moves between devices by JAX's collectives and lax.ppermute only.
A program may use at most 128 MiB of HBM per device.

```python
import math
import jax
import jax.numpy as jnp
import numpy as np
from jax import lax

D = 2048
FF = 768
TOK_DEV = 128
TOP = 2
SLOTS = 32
EXPERTS = 16
CAP = 10
GROUP = 4096
TOKENS = 32768
N_DP = 8
N_EXPERT = 32


def draw_placement(key, part):
    key = jax.random.fold_in(key, 11)
    first, second, third, fourth = jax.random.split(key, 4)
    every_one = jax.random.permutation(first, EXPERTS).astype(jnp.int32)
    popular = jax.random.permutation(second, EXPERTS)[:2].astype(jnp.int32)
    picks = jax.random.randint(third, (N_EXPERT - EXPERTS,), 0, 2)
    table = jnp.concatenate([every_one, popular[picks]])
    order = jax.random.permutation(fourth, N_EXPERT)
    return table[order].astype(jnp.int32)


def level_of(stream_key, dims, pieces, smallest, high):
    loudness = 1.0
    for dim, parts in pieces:
        steps = jax.random.uniform(jax.random.fold_in(jax.random.fold_in(stream_key, 6), dim), (parts,), jnp.float32, smallest / len(pieces), high / len(pieces))
        loudness = loudness * jnp.repeat(jnp.exp(steps), dims[dim] // parts).reshape((-1,) + (1,) * (len(dims) - 1 - dim))
    return loudness


def assign_block(stream_key, own, number, rows, amount, top, reach, slope):
    ranking = jax.random.permutation(stream_key, amount)
    packed, ordinary = load_shares(amount, rows * top, reach, slope, True), load_shares(amount, rows * top, reach, slope, False)
    places = jnp.arange(amount)

    def named(lengths, rotation):
        used = int((lengths > 0).sum())
        fixed = max(1, used // 4)
        shifted = fixed + (places - fixed + rotation * (used - fixed)) % max(1, amount - fixed)
        return jnp.zeros((amount,), jnp.int32).at[ranking[jnp.where(places < fixed, places, shifted)]].set(jnp.asarray(lengths, jnp.int32))

    lengths = jnp.where(number % 4 == 0, named(packed, number // 4), named(ordinary, number - number // 4 - 1))
    mixed = jax.random.permutation(jax.random.fold_in(own, 3), amount)
    source_of, sink = mixed[0:amount // 2 * 2:2], mixed[1:amount // 2 * 2:2]
    slack = jnp.minimum(lengths[source_of] - 1, reach - lengths[sink]) // 2
    slack = jnp.where((source_of == ranking[0]) | (sink == ranking[0]) | (lengths[sink] == 0), 0, jnp.maximum(slack, 0))
    shifted = jax.random.randint(jax.random.fold_in(own, 4), (amount // 2,), 0, 1 << 20) % (slack + 1)
    lengths = lengths.at[source_of].add(-shifted).at[sink].add(shifted)
    members = jnp.searchsorted(jnp.cumsum(lengths), jnp.arange(rows * top), side="right").astype(jnp.int32)
    listing = members.reshape(top, rows).T
    listing = listing[jax.random.permutation(jax.random.fold_in(own, 1), rows)]
    rotation = jax.random.randint(jax.random.fold_in(own, 2), (rows, 1), 0, top)
    return jnp.take_along_axis(listing, (jnp.arange(top)[None, :] + rotation) % top, axis=1)


def load_shares(count, total, reach, lean, full):
    weights = [(1 << 20) // math.isqrt(rank ** lean) + 1 for rank in range(1, count + 1)]
    largest = reach if full else min(reach, max(-(-total // count), total * weights[0] // sum(weights)))
    least = 1 if total - largest >= count - 1 else 0
    holding, spare = [largest] + [least] * (count - 1), total - largest - least * (count - 1)
    while spare > 0:
        free = [i for i in range(1, count) if holding[i] < largest] or [i for i in range(1, count) if holding[i] < reach]
        mass, budget = sum([weights[i] for i in free]), spare
        for i in free:
            more = min(reach - holding[i], max(1, budget * weights[i] // mass), spare)
            holding[i] = holding[i] + more
            spare = spare - more
    return np.array(holding)


def centred(rng, dims, width, bound, cuts=(), kind=jnp.bfloat16):
    drawn = jax.random.normal(rng, dims, jnp.float32) * width
    if len(cuts) > 0:
        drawn = level_of(rng, dims, cuts, -0.22, 0.18) * drawn
    return jnp.clip(drawn, min=-bound, max=bound).astype(kind)


def setup_inputs(seed: int = 0) -> dict:
    key_list = jax.random.split(jax.random.key(seed), 9)
    tokens = centred(key_list[0], (TOKENS, D), 1.0, 6.0, ((0, 256),))
    cotangent = centred(key_list[1], (TOKENS, D), 1.0, 6.0, ((0, 256),))
    routed_slots_keys = jax.random.split(jax.random.fold_in(key_list[2], 1), TOKENS // TOK_DEV)
    routed_slots_turns = jax.random.permutation(jax.random.fold_in(key_list[2], 3), TOKENS // TOK_DEV)
    routed_slots = jax.vmap(lambda own, number: assign_block(jax.random.fold_in(key_list[2], 2), own, number, TOK_DEV, SLOTS, TOP, CAP, 2))(routed_slots_keys, routed_slots_turns).reshape((TOKENS, TOP))
    route_probs = jnp.clip(jnp.exp(math.log(1.0) - 2.9996462 * jax.random.uniform(key_list[3], (TOKENS, TOP), jnp.float32) ** level_of(key_list[3], (TOKENS, TOP), ((0, 256),), -0.2, 0.2)), 0.049804688, 1.0).astype(jnp.bfloat16)
    placement = draw_placement(jax.random.fold_in(key_list[8], 71), 0)
    w_gate = centred(key_list[5], (EXPERTS, FF, D), D ** -0.5, 0.125, ((1, 32),))
    w_up = centred(key_list[6], (EXPERTS, FF, D), D ** -0.5, 0.125, ((1, 32),))
    w_down = centred(key_list[7], (EXPERTS, FF, D), FF ** -0.5, 0.21875, ((1, 32),))
    return {"tokens": tokens, "cotangent": cotangent, "routed_slots": routed_slots, "route_probs": route_probs, "placement": placement, "w_gate": w_gate, "w_up": w_up, "w_down": w_down}


def expert_rows(in_rows, cot_rows, prob_rows, gate_slab, up_slab, down_slab):
    gate_pre = jnp.dot(in_rows, gate_slab.T, preferred_element_type=jnp.float32)
    up_pre = jnp.dot(in_rows, up_slab.T, preferred_element_type=jnp.float32)
    sigma = jax.nn.sigmoid(gate_pre)
    swish = gate_pre * sigma
    hidden = (swish * up_pre).astype(jnp.bfloat16)
    out_rows = jnp.dot(hidden, down_slab, preferred_element_type=jnp.float32)
    prob_grad = jnp.sum(out_rows * cot_rows.astype(jnp.float32), axis=1).astype(jnp.bfloat16)
    scaled = (prob_rows.astype(jnp.float32)[:, None] * cot_rows.astype(jnp.float32)).astype(jnp.bfloat16)
    hidden_grad = jnp.dot(scaled, down_slab.T, preferred_element_type=jnp.float32)
    gate_grad = (hidden_grad * up_pre * sigma * (1.0 + gate_pre * (1.0 - sigma))).astype(jnp.bfloat16)
    up_grad = (hidden_grad * swish).astype(jnp.bfloat16)
    pair_grad = (jnp.dot(gate_grad, gate_slab, preferred_element_type=jnp.float32)
                 + jnp.dot(up_grad, up_slab, preferred_element_type=jnp.float32)).astype(jnp.bfloat16)
    part_gate = jnp.dot(gate_grad.T, in_rows, preferred_element_type=jnp.float32).astype(jnp.bfloat16)
    part_up = jnp.dot(up_grad.T, in_rows, preferred_element_type=jnp.float32).astype(jnp.bfloat16)
    part_down = jnp.dot(hidden.T, scaled, preferred_element_type=jnp.float32).astype(jnp.bfloat16)
    return pair_grad, prob_grad, part_gate, part_up, part_down


def reference(tokens, cotangent, routed_slots, route_probs, placement, w_gate, w_up, w_down):
    buffer_rows = N_EXPERT * CAP
    pair_count = GROUP * TOP
    model_width = tokens.shape[1]
    grad_total = jnp.zeros((EXPERTS, 3, FF, model_width), jnp.float32)
    token_parts = []
    prob_parts = []
    for group_index in range(N_DP):
        first = group_index * GROUP
        group_tokens = tokens[first:first + GROUP]
        group_cot = cotangent[first:first + GROUP]
        flat_slots = routed_slots[first:first + GROUP].reshape(pair_count)
        flat_probs = route_probs[first:first + GROUP].reshape(pair_count)

        def visit(carry, slot_index):
            pair_grads, prob_grads, grads = carry
            found = jnp.nonzero(flat_slots == slot_index, size=buffer_rows, fill_value=pair_count)[0].astype(jnp.int32)
            valid = found < pair_count
            safe = jnp.minimum(found, pair_count - 1)
            token_index = safe // TOP
            zero = jnp.zeros((), jnp.bfloat16)
            in_rows = jnp.where(valid[:, None], group_tokens[token_index], zero)
            cot_rows = jnp.where(valid[:, None], group_cot[token_index], zero)
            prob_rows = jnp.where(valid, flat_probs[safe], zero)
            expert = placement[slot_index]
            pair_grad, prob_grad, part_gate, part_up, part_down = expert_rows(
                in_rows, cot_rows, prob_rows, w_gate[expert], w_up[expert], w_down[expert])
            pair_grads = pair_grads.at[found].set(pair_grad.astype(jnp.float32), mode="drop")
            prob_grads = prob_grads.at[found].set(prob_grad.astype(jnp.float32), mode="drop")
            stacked = jnp.stack([part_gate, part_up, part_down]).astype(jnp.float32)
            grads = grads.at[expert].add(stacked)
            return (pair_grads, prob_grads, grads), None

        start = (jnp.zeros((pair_count, model_width), jnp.float32), jnp.zeros((pair_count,), jnp.float32), grad_total)
        (pair_grads, prob_grads, grad_total), _ = lax.scan(visit, start, jnp.arange(N_EXPERT, dtype=jnp.int32))
        token_parts.append(jnp.sum(pair_grads.reshape(GROUP, TOP, model_width), axis=1).astype(jnp.bfloat16))
        prob_parts.append(prob_grads.reshape(GROUP, TOP).astype(jnp.bfloat16))
    grad_all = grad_total.astype(jnp.bfloat16)
    return (jnp.concatenate(token_parts, axis=0), jnp.concatenate(prob_parts, axis=0),
            grad_all[:, 0], grad_all[:, 1], grad_all[:, 2])
```

```python
import functools

import jax
import jax.numpy as jnp
from jax import lax
from jax.experimental import pallas as pl
from jax.experimental.pallas import tpu as pltpu
from jax.sharding import PartitionSpec as P

F32 = jnp.float32
BF16 = jnp.bfloat16
I32 = jnp.int32
CAPACITY = 10
MAIN = 8
LANES = 128


def params():
    return pltpu.CompilerParams(vmem_limit_bytes=50 * 1024 * 1024)


def iota(shape, dim):
    return lax.broadcasted_iota(I32, shape, dim)


def ones_where(mask):
    return jnp.where(mask, 1.0, 0.0).astype(BF16)


def matmul(a, b):
    return jnp.dot(a, b, preferred_element_type=F32)


def matmul_t(a, b):
    return lax.dot_general(a, b, (((1,), (1,)), ((), ())), preferred_element_type=F32)


def pick_kernel(index_ref, gate_ref, up_ref, down_ref, out_ref):
    def one(slot, carry):
        expert = index_ref[1 + slot]
        out_ref[slot, 0] = gate_ref[expert]
        out_ref[slot, 1] = up_ref[expert]
        out_ref[slot, 2] = down_ref[expert]
        return carry

    lax.fori_loop(0, out_ref.shape[0], one, 0)


def pick(index, w_gate, w_up, w_down, slots, columns):
    experts, share, _ = w_gate.shape
    spec = pl.BlockSpec((experts, share, columns), lambda i, index: (0, 0, index[0]))
    return pl.pallas_call(
        pick_kernel,
        grid_spec=pltpu.PrefetchScalarGridSpec(
            num_scalar_prefetch=1,
            grid=(1,),
            in_specs=[spec] * 3,
            out_specs=pl.BlockSpec((slots, 3, share, columns), lambda i, index: (0, 0, 0, 0)),
        ),
        out_shape=jax.ShapeDtypeStruct((slots, 3, share, columns), BF16),
        compiler_params=params(),
    )(index, w_gate, w_up, w_down)


def pack_kernel(slots_ref, probs_ref, tok_ref, cot_ref, out_ref):
    tokens, width = tok_ref.shape
    count = out_ref.shape[0] // (2 * MAIN)
    quarter = width // 4
    first, second = slots_ref[0:1, :], slots_ref[1:2, :]
    row = iota((count, tokens), 0)
    in_first, in_second = first == row, second == row
    before = matmul(
        ones_where(in_first | in_second),
        ones_where(iota((tokens, tokens), 0) < iota((tokens, tokens), 1)),
    )
    rank_first = jnp.sum(jnp.where(in_first, before, 0.0), axis=0, keepdims=True).astype(I32)
    rank_second = jnp.sum(jnp.where(in_second, before, 0.0), axis=0, keepdims=True).astype(I32)
    code_first = first * 16 + rank_first
    code_second = second * 16 + rank_second

    row = iota((count * MAIN, tokens), 0)
    code = (row >> 3) * 16 + (row & 7)
    chosen = ones_where((code == code_first) | (code == code_second))
    for part in range(4):
        at = pl.ds(part * quarter, quarter)
        tok_rows = matmul(chosen, tok_ref[:, at]).reshape(count, MAIN, quarter)
        cot_rows = matmul(chosen, cot_ref[:, at]).reshape(count, MAIN, quarter)
        both = jnp.concatenate([tok_rows[:, None], cot_rows[:, None]], axis=1)
        out_ref[:, at] = both.reshape(count * 2 * MAIN, quarter).astype(BF16)

    row = iota((count * 2 * MAIN, tokens), 0)
    code = (row >> 4) * 16 + MAIN + (row & 1)
    hit = (code == code_first) | (code == code_second)
    total = jnp.zeros((count * 2 * MAIN, quarter), F32)
    for part in range(4):
        here = hit & (((row >> 2) & 3) == part)
        is_cot = ((row >> 1) & 1) == 1
        at = pl.ds(part * quarter, quarter)
        total += matmul(ones_where(here & jnp.logical_not(is_cot)), tok_ref[:, at])
        total += matmul(ones_where(here & is_cot), cot_ref[:, at])
    out_ref[:, pl.ds(width, quarter)] = total.astype(BF16)

    inner = row & 15
    rank = jnp.where(inner >= 8, inner - 8, jnp.where(inner < 2, inner + 8, 15))
    code = (row >> 4) * 16 + rank
    weight = jnp.sum(
        jnp.where(code == code_first, probs_ref[0:1, :], 0.0)
        + jnp.where(code == code_second, probs_ref[1:2, :], 0.0),
        axis=1,
        keepdims=True,
    )
    out_ref[:, pl.ds(width + quarter, LANES)] = jnp.broadcast_to(
        weight, (count * 2 * MAIN, LANES)
    ).astype(BF16)


def pack(slots_t, probs_t, tokens, cotangent, slots):
    width = tokens.shape[1]
    return pl.pallas_call(
        pack_kernel,
        out_shape=jax.ShapeDtypeStruct((slots * 2 * MAIN, width + width // 4 + LANES), BF16),
        compiler_params=params(),
    )(slots_t, probs_t, tokens, cotangent)


def hidden_kernel(
    main_ref, rest_ref, prob_ref, w_ref,
    part_ref, gate_grad_ref, up_grad_ref, hidden_ref, cot_ref,
    gate_acc, up_acc, down_acc, tok_keep, scaled_keep, weight_keep, gate_t, up_t, hidden_t,
):
    phase, step = pl.program_id(0), pl.program_id(1)
    rows = main_ref.shape[0]
    count = rows // 16
    mains, rests = count * MAIN, count * 2
    total = mains + rests
    columns = main_ref.shape[1]
    padded = tok_keep.shape[1]

    @pl.when((phase == 0) & (step == 0))
    def _():
        block = prob_ref[...].astype(F32).reshape(count, 2, MAIN, LANES)
        row, column = iota((rests, rows), 0), iota((rests, rows), 1)
        found = ones_where(column == (row >> 1) * 16 + (row & 1))
        weight_keep[0:mains, :] = block[:, 1].reshape(mains, LANES)
        weight_keep[mains:total, :] = matmul(found, prob_ref[...])
        gate_acc[...] = jnp.zeros_like(gate_acc)
        up_acc[...] = jnp.zeros_like(up_acc)
        down_acc[...] = jnp.zeros_like(down_acc)

    @pl.when(phase == 0)
    def _():
        block = main_ref[...].astype(F32).reshape(count, 2, MAIN, columns)
        row, column = iota((2 * rests, rows), 0), iota((2 * rests, rows), 1)
        is_cot = jnp.where(row >= rests, 1, 0)
        inner = row - is_cot * rests
        source = (inner >> 1) * 16 + (step // 2) * 4 + is_cot * 2 + (inner & 1)
        rest = matmul(ones_where(column == source), rest_ref[...])
        tok = jnp.concatenate([block[:, 0].reshape(mains, columns), rest[:rests]], axis=0).astype(BF16)
        cot = jnp.concatenate([block[:, 1].reshape(mains, columns), rest[rests:]], axis=0)
        scaled = (weight_keep[:, 0:1] * cot).astype(BF16)
        empty = jnp.zeros((padded - total, columns), BF16)
        tok_keep[step] = jnp.concatenate([tok, empty], axis=0)
        scaled_keep[step] = jnp.concatenate([scaled, empty], axis=0)
        cot_ref[0] = cot.astype(BF16)
        gate_acc[...] += matmul_t(tok, w_ref[0, 0])
        up_acc[...] += matmul_t(tok, w_ref[0, 1])
        down_acc[...] += matmul_t(scaled, w_ref[0, 2])

    @pl.when((phase == 1) & (step == 0))
    def _():
        hidden_units = gate_acc.shape[1]
        for start in range(0, padded, 128):
            size = min(128, total - start)
            at = pl.ds(start, size)
            gate_pre, up_pre, hidden_grad = gate_acc[at, :], up_acc[at, :], down_acc[at, :]
            sigma = jax.nn.sigmoid(gate_pre)
            swish = gate_pre * sigma
            hidden = swish * up_pre
            gate_grad = hidden_grad * up_pre * sigma * (1.0 + gate_pre * (1.0 - sigma))
            up_grad = hidden_grad * swish
            for value, out, out_t in (
                (hidden, hidden_ref, hidden_t),
                (gate_grad, gate_grad_ref, gate_t),
                (up_grad, up_grad_ref, up_t),
            ):
                out[at, :] = value.astype(BF16)
                if size < 128:
                    value = jnp.concatenate([value, jnp.zeros((128 - size, hidden_units), F32)], axis=0)
                out_t[:, pl.ds(start, 128)] = value.T.astype(BF16)

    @pl.when(phase == 1)
    def _():
        part_ref[0, 0] = matmul(gate_t[...], tok_keep[step]).astype(BF16)
        part_ref[0, 1] = matmul(up_t[...], tok_keep[step]).astype(BF16)
        part_ref[0, 2] = matmul(hidden_t[...], scaled_keep[step]).astype(BF16)


def hidden_layer(got, weights):
    steps, _, hidden, columns = weights.shape
    rows = got.shape[0]
    total = rows // 16 * CAPACITY
    padded = -(-total // 128) * 128
    width = steps * columns
    quarter = width // 4
    per_quarter = quarter // columns

    def held(shape):
        return pl.BlockSpec(shape, lambda phase, step: (0,) * len(shape))

    return pl.pallas_call(
        hidden_kernel,
        grid=(2, steps),
        in_specs=[
            pl.BlockSpec((rows, columns), lambda phase, step: (0, jnp.where(phase == 0, step, steps - 1))),
            pl.BlockSpec(
                (rows, columns),
                lambda phase, step: (0, jnp.where(phase == 0, steps + step % per_quarter, steps + per_quarter - 1)),
            ),
            pl.BlockSpec((rows, LANES), lambda phase, step: (0, (width + quarter) // LANES)),
            pl.BlockSpec(
                (1, 3, hidden, columns), lambda phase, step: (jnp.where(phase == 0, step, steps - 1), 0, 0, 0)
            ),
        ],
        out_specs=[
            pl.BlockSpec((1, 3, hidden, columns), lambda phase, step: (jnp.where(phase == 0, 0, step), 0, 0, 0)),
            held((total, hidden)),
            held((total, hidden)),
            held((total, hidden)),
            pl.BlockSpec((1, total, columns), lambda phase, step: (jnp.where(phase == 0, step, steps - 1), 0, 0)),
        ],
        out_shape=[
            jax.ShapeDtypeStruct((steps, 3, hidden, columns), BF16),
            jax.ShapeDtypeStruct((total, hidden), BF16),
            jax.ShapeDtypeStruct((total, hidden), BF16),
            jax.ShapeDtypeStruct((total, hidden), BF16),
            jax.ShapeDtypeStruct((steps, total, columns), BF16),
        ],
        scratch_shapes=[
            pltpu.VMEM((total, hidden), F32),
            pltpu.VMEM((total, hidden), F32),
            pltpu.VMEM((total, hidden), F32),
            pltpu.VMEM((steps, padded, columns), BF16),
            pltpu.VMEM((steps, padded, columns), BF16),
            pltpu.VMEM((total, LANES), F32),
            pltpu.VMEM((hidden, padded), BF16),
            pltpu.VMEM((hidden, padded), BF16),
            pltpu.VMEM((hidden, padded), BF16),
        ],
        compiler_params=params(),
    )(got, got, got, weights)


def pair_kernel(gate_grad_ref, up_grad_ref, hidden_ref, cot_ref, w_ref, out_ref, rest_acc, prob_acc):
    step = pl.program_id(0)
    steps = pl.num_programs(0)
    columns = w_ref.shape[3]
    mains = out_ref.shape[0]
    count = mains // MAIN
    rests = count * 2
    width = cot_ref.shape[2] * steps

    @pl.when(step == 0)
    def _():
        rest_acc[...] = jnp.zeros_like(rest_acc)
        prob_acc[...] = jnp.zeros_like(prob_acc)

    gate_w, up_w, down_w = w_ref[0, 0], w_ref[0, 1], w_ref[0, 2]
    grad = (matmul(gate_grad_ref[...], gate_w) + matmul(up_grad_ref[...], up_w)).astype(BF16)
    out_ref[:, pl.ds(pl.multiple_of(step * columns, columns), columns)] = grad[:mains]
    row, column = iota((mains, rests), 0), iota((mains, rests), 1)
    inner = row & 7
    placed = ones_where(((inner >> 1) == step // 2) & (column == (row >> 3) * 2 + (inner & 1)))
    rest_acc[step % 2] += matmul(placed, grad[mains:])
    prob_acc[...] += matmul(hidden_ref[...], down_w) * cot_ref[0].astype(F32)

    @pl.when(step == steps - 1)
    def _():
        out_ref[:, pl.ds(width, columns)] = rest_acc[0].astype(BF16)
        out_ref[:, pl.ds(width + columns, columns)] = rest_acc[1].astype(BF16)
        prob = jnp.broadcast_to(
            jnp.sum(prob_acc[...], axis=1, keepdims=True), (mains + rests, LANES)
        ).astype(BF16)
        placed = ones_where((inner < 2) & (column == (row >> 3) * 2 + inner))
        moved = matmul(placed, prob[mains:])
        lane = iota((mains, LANES), 1)
        out_ref[:, pl.ds(width + 2 * columns, LANES)] = jnp.where(
            lane < LANES // 2, prob[:mains].astype(F32), moved
        ).astype(BF16)


def pair_layer(gate_grad, up_grad, hidden, cot, weights):
    steps, _, units, columns = weights.shape
    total = gate_grad.shape[0]
    mains = total // CAPACITY * MAIN
    width = steps * columns
    lanes = width + width // 4 + LANES
    held = pl.BlockSpec((total, units), lambda step: (0, 0))
    return pl.pallas_call(
        pair_kernel,
        grid=(steps,),
        in_specs=[
            held,
            held,
            held,
            pl.BlockSpec((1, total, columns), lambda step: (step, 0, 0)),
            pl.BlockSpec((1, 3, units, columns), lambda step: (step, 0, 0, 0)),
        ],
        out_specs=pl.BlockSpec((mains, lanes), lambda step: (0, 0)),
        out_shape=jax.ShapeDtypeStruct((mains, lanes), BF16),
        scratch_shapes=[
            pltpu.VMEM((2, mains, columns), F32),
            pltpu.VMEM((total, columns), F32),
        ],
        compiler_params=params(),
    )(gate_grad, up_grad, hidden, cot, weights)


def combine_kernel(slots_ref, back_ref, token_ref, prob_ref):
    tokens, width = token_ref.shape
    mains = back_ref.shape[0]
    count = mains // MAIN
    quarter = width // 4
    first, second = slots_ref[:, 0:1], slots_ref[:, 1:2]
    column = iota((tokens, count), 1)
    in_first, in_second = first == column, second == column
    before = matmul(
        ones_where(iota((tokens, tokens), 0) > iota((tokens, tokens), 1)),
        ones_where(in_first | in_second),
    )
    rank_first = jnp.sum(jnp.where(in_first, before, 0.0), axis=1, keepdims=True).astype(I32)
    rank_second = jnp.sum(jnp.where(in_second, before, 0.0), axis=1, keepdims=True).astype(I32)
    code_first = first * 16 + rank_first
    code_second = second * 16 + rank_second

    cell = iota((tokens, mains), 1)
    code = (cell >> 3) * 16 + (cell & 7)
    main_first, main_second = code == code_first, code == code_second
    chosen = ones_where(main_first | main_second)
    code = (cell >> 3) * 16 + MAIN + (cell & 1)
    rest_hit = (code == code_first) | (code == code_second)
    rest_rows = back_ref[:, pl.ds(width, quarter)]
    for part in range(4):
        at = pl.ds(part * quarter, quarter)
        picked = ones_where(rest_hit & (((cell >> 1) & 3) == part))
        token_ref[:, at] = (matmul(chosen, back_ref[:, at]) + matmul(picked, rest_rows)).astype(BF16)

    probs = back_ref[:, pl.ds(width + quarter, LANES)]
    inner = cell & 7
    code = jnp.where(inner < 2, (cell >> 3) * 16 + MAIN + inner, -1)
    found = []
    for main_hit, mine in ((main_first, code_first), (main_second, code_second)):
        of_main = matmul(ones_where(main_hit), probs)[:, 0:1]
        of_rest = matmul(ones_where(code == mine), probs)[:, LANES // 2 : LANES // 2 + 1]
        found.append(of_main + of_rest)
    prob_ref[...] = jnp.concatenate(found, axis=1).astype(BF16)


def combine(routed_slots, back, tokens, width):
    return pl.pallas_call(
        combine_kernel,
        out_shape=[
            jax.ShapeDtypeStruct((tokens, width), BF16),
            jax.ShapeDtypeStruct((tokens, 2), BF16),
        ],
        compiler_params=params(),
    )(routed_slots, back)


def fold_kernel(placement_ref, part_ref, gate_ref, up_ref, down_ref, total):
    total[...] = jnp.zeros_like(total)

    def one(slot, carry):
        expert = placement_ref[slot]
        total[expert] += part_ref[slot].astype(F32)
        return carry

    lax.fori_loop(0, part_ref.shape[0], one, 0)
    gate_ref[...] = total[:, 0].astype(BF16)
    up_ref[...] = total[:, 1].astype(BF16)
    down_ref[...] = total[:, 2].astype(BF16)


def fold(placement, parts, experts):
    slots, _, share, columns = parts.shape
    spec = pl.BlockSpec((experts, share, columns), lambda i, placement: (0, 0, 0))
    return pl.pallas_call(
        fold_kernel,
        grid_spec=pltpu.PrefetchScalarGridSpec(
            num_scalar_prefetch=1,
            grid=(1,),
            in_specs=[pl.BlockSpec((slots, 3, share, columns), lambda i, placement: (0, 0, 0, 0))],
            out_specs=[spec] * 3,
            scratch_shapes=[pltpu.VMEM((experts, 3, share, columns), F32)],
        ),
        out_shape=[jax.ShapeDtypeStruct((experts, share, columns), BF16)] * 3,
        compiler_params=params(),
    )(placement, parts)


def over_expert(value):
    return lax.all_to_all(value, "expert", split_axis=0, concat_axis=0, tiled=True)


def on_device(tokens, cotangent, routed_slots, route_probs, placement, w_gate, w_up, w_down):
    slots = lax.axis_size("expert")
    groups = lax.axis_size("dp")
    token_rows, width = tokens.shape
    columns = width // groups
    experts, share, _ = w_gate.shape
    hidden = share * slots

    index = jnp.concatenate([lax.axis_index("dp").astype(I32)[None], placement])
    wanted = pick(index, w_gate, w_up, w_down, slots, columns)
    payload = pack(routed_slots.T, route_probs.T.astype(F32), tokens, cotangent, slots)
    mine = over_expert(wanted)
    mine, payload = lax.optimization_barrier((mine, payload))
    mine = mine.transpose(1, 0, 2, 3).reshape(3, hidden, columns)
    weights = lax.all_gather(mine, "dp", axis=0)
    got = over_expert(payload.reshape(slots, 2 * MAIN, -1)).reshape(payload.shape)

    parts, gate_grad, up_grad, hidden_rows, cot = hidden_layer(got, weights)
    summed = lax.psum_scatter(parts, "dp", scatter_dimension=0)
    pairs = pair_layer(gate_grad, up_grad, hidden_rows, cot, weights)
    back = over_expert(pairs.reshape(slots, MAIN, -1)).reshape(pairs.shape)
    token_grad, prob_grad = combine(routed_slots, back, token_rows, width)

    homeward = summed.reshape(3, slots, share, columns).transpose(1, 0, 2, 3)
    grads = fold(placement, over_expert(homeward), experts)
    return (token_grad, prob_grad, *grads)


def solution(mesh):
    placed = (
        P(("dp", "expert"), None),
        P(("dp", "expert"), None),
        P(("dp", "expert"), None),
        P(("dp", "expert"), None),
        P(),
        P(None, "expert", None),
        P(None, "expert", None),
        P(None, "expert", None),
    )
    return jax.shard_map(
        on_device,
        mesh=mesh,
        in_specs=placed,
        out_specs=(
            P(("dp", "expert"), None),
            P(("dp", "expert"), None),
            P(None, "expert", "dp"),
            P(None, "expert", "dp"),
            P(None, "expert", "dp"),
        ),
        check_vma=False,
    )
```

```python
import functools

import jax
import jax.numpy as jnp
from jax import lax
from jax.experimental import pallas as pl
from jax.experimental.pallas import tpu as pltpu
from jax.sharding import PartitionSpec as P

F32 = jnp.float32
BF16 = jnp.bfloat16
I32 = jnp.int32
CAPACITY = 10
MAIN = 8
LANES = 128


def params():
    return pltpu.CompilerParams(vmem_limit_bytes=50 * 1024 * 1024)


def iota(shape, dim):
    return lax.broadcasted_iota(I32, shape, dim)


def ones_where(mask):
    return jnp.where(mask, 1.0, 0.0).astype(BF16)


def matmul(a, b):
    return jnp.dot(a, b, preferred_element_type=F32)


def matmul_t(a, b):
    return lax.dot_general(a, b, (((1,), (1,)), ((), ())), preferred_element_type=F32)


def pick_kernel(index_ref, gate_ref, up_ref, down_ref, out_ref):
    def one(slot, carry):
        expert = index_ref[1 + slot]
        out_ref[slot, 0] = gate_ref[expert]
        out_ref[slot, 1] = up_ref[expert]
        out_ref[slot, 2] = down_ref[expert]
        return carry

    lax.fori_loop(0, out_ref.shape[0], one, 0)


def pick(index, w_gate, w_up, w_down, slots, columns):
    experts, share, _ = w_gate.shape
    spec = pl.BlockSpec((experts, share, columns), lambda i, index: (0, 0, index[0]))
    return pl.pallas_call(
        pick_kernel,
        grid_spec=pltpu.PrefetchScalarGridSpec(
            num_scalar_prefetch=1,
            grid=(1,),
            in_specs=[spec] * 3,
            out_specs=pl.BlockSpec((slots, 3, share, columns), lambda i, index: (0, 0, 0, 0)),
        ),
        out_shape=jax.ShapeDtypeStruct((slots, 3, share, columns), BF16),
        compiler_params=params(),
    )(index, w_gate, w_up, w_down)


def pack_kernel(slots_ref, probs_ref, tok_ref, cot_ref, out_ref):
    tokens, width = tok_ref.shape
    count = out_ref.shape[0] // (2 * MAIN)
    quarter = width // 4
    first, second = slots_ref[0:1, :], slots_ref[1:2, :]
    row = iota((count, tokens), 0)
    in_first, in_second = first == row, second == row
    before = matmul(
        ones_where(in_first | in_second),
        ones_where(iota((tokens, tokens), 0) < iota((tokens, tokens), 1)),
    )
    rank_first = jnp.sum(jnp.where(in_first, before, 0.0), axis=0, keepdims=True).astype(I32)
    rank_second = jnp.sum(jnp.where(in_second, before, 0.0), axis=0, keepdims=True).astype(I32)
    code_first = first * 16 + rank_first
    code_second = second * 16 + rank_second

    def look_up(code):
        hit_first, hit_second = code == code_first, code == code_second
        weight = jnp.sum(
            jnp.where(hit_first, probs_ref[0:1, :], 0.0) + jnp.where(hit_second, probs_ref[1:2, :], 0.0),
            axis=1,
            keepdims=True,
        )
        return hit_first | hit_second, weight

    row = iota((count * MAIN, tokens), 0)
    hit, weight = look_up((row >> 3) * 16 + (row & 7))
    chosen = ones_where(hit)
    for part in range(4):
        at = pl.ds(part * quarter, quarter)
        tok_rows = matmul(chosen, tok_ref[:, at]).reshape(count, MAIN, quarter)
        cot_rows = (weight * matmul(chosen, cot_ref[:, at])).reshape(count, MAIN, quarter)
        both = jnp.concatenate([tok_rows[:, None], cot_rows[:, None]], axis=1)
        out_ref[:, at] = both.reshape(count * 2 * MAIN, quarter).astype(BF16)

    row = iota((count * 2 * MAIN, tokens), 0)
    hit, weight = look_up((row >> 4) * 16 + MAIN + (row & 1))
    is_cot = ((row >> 1) & 1) == 1
    tok_rows = jnp.zeros((count * 2 * MAIN, quarter), F32)
    cot_rows = jnp.zeros((count * 2 * MAIN, quarter), F32)
    for part in range(4):
        here = hit & (((row >> 2) & 3) == part)
        at = pl.ds(part * quarter, quarter)
        tok_rows += matmul(ones_where(here & jnp.logical_not(is_cot)), tok_ref[:, at])
        cot_rows += matmul(ones_where(here & is_cot), cot_ref[:, at])
    out_ref[:, pl.ds(width, quarter)] = (tok_rows + weight * cot_rows).astype(BF16)


def pack(slots_t, probs_t, tokens, cotangent, slots):
    width = tokens.shape[1]
    return pl.pallas_call(
        pack_kernel,
        out_shape=jax.ShapeDtypeStruct((slots * 2 * MAIN, width + width // 4), BF16),
        compiler_params=params(),
    )(slots_t, probs_t, tokens, cotangent)


def hidden_kernel(
    got_ref, w_ref,
    part_ref, gate_grad_ref, up_grad_ref, hidden_ref, scaled_ref,
    got_buf, rest_buf, w_buf, part_buf, tok_keep, scaled_keep, gate_acc, up_acc, down_acc, gate_t, up_t, hidden_t,
    got_sem, rest_sem, w_sem, part_sem,
):
    steps, rows, columns = got_buf.shape
    count = rows // 16
    mains, rests = count * MAIN, count * 2
    total = mains + rests
    padded = tok_keep.shape[1]
    units = gate_acc.shape[1]
    width = steps * columns

    rest_copy = pltpu.make_async_copy(got_ref.at[:, pl.ds(width, width // 4)], rest_buf, rest_sem)
    rest_copy.start()
    got_copies, w_copies = [], []
    for step in range(steps):
        got_copies.append(
            pltpu.make_async_copy(got_ref.at[:, pl.ds(step * columns, columns)], got_buf.at[step], got_sem.at[step])
        )
        w_copies.append(pltpu.make_async_copy(w_ref.at[step], w_buf.at[step], w_sem.at[step]))
        got_copies[step].start()
        w_copies[step].start()

    row, column = iota((2 * rests, rows), 0), iota((2 * rests, rows), 1)
    second = jnp.where(row >= rests, 1, 0)
    inner = row - second * rests
    source = (inner >> 1) * 16 + second * 2 + (inner & 1)
    rest_copy.wait()
    per_quarter = width // 4 // columns
    empty = jnp.zeros((padded - total, columns), BF16)
    for step in range(steps):
        got_copies[step].wait()
        block = got_buf[step].astype(F32).reshape(count, 2, MAIN, columns)
        found = ones_where(column == source + 4 * (step // per_quarter))
        rest = matmul(found, rest_buf[:, pl.ds(step % per_quarter * columns, columns)])
        tok = jnp.concatenate([block[:, 0].reshape(mains, columns), rest[:rests]], axis=0).astype(BF16)
        scaled = jnp.concatenate([block[:, 1].reshape(mains, columns), rest[rests:]], axis=0).astype(BF16)
        tok_keep[step, 0:total] = tok
        tok_keep[step, total:padded] = empty
        scaled_keep[step, 0:total] = scaled
        scaled_keep[step, total:padded] = empty
        scaled_ref[step] = scaled
        w_copies[step].wait()
        terms = (
            (gate_acc, matmul_t(tok, w_buf[step, 0])),
            (up_acc, matmul_t(tok, w_buf[step, 1])),
            (down_acc, matmul_t(scaled, w_buf[step, 2])),
        )
        for acc, term in terms:
            acc[...] = term if step == 0 else acc[...] + term

    for start in range(0, padded, 128):
        size = min(128, total - start)
        at = pl.ds(start, size)
        gate_pre, up_pre, hidden_grad = gate_acc[at, :], up_acc[at, :], down_acc[at, :]
        sigma = jax.nn.sigmoid(gate_pre)
        swish = gate_pre * sigma
        hidden = swish * up_pre
        gate_grad = hidden_grad * up_pre * sigma * (1.0 + gate_pre * (1.0 - sigma))
        up_grad = hidden_grad * swish
        for value, out, out_t in (
            (hidden, hidden_ref, hidden_t),
            (gate_grad, gate_grad_ref, gate_t),
            (up_grad, up_grad_ref, up_t),
        ):
            out[at, :] = value.astype(BF16)
            if size < 128:
                value = jnp.concatenate([value, jnp.zeros((128 - size, units), F32)], axis=0)
            out_t[:, pl.ds(start, 128)] = value.T.astype(BF16)

    part_copies = []
    slots, share = part_buf.shape[1], part_buf.shape[3]
    for step in range(steps):
        for matrix, (left, right) in enumerate(((gate_t, tok_keep), (up_t, tok_keep), (hidden_t, scaled_keep))):
            part = matmul(left[...], right[step])
            part_buf[step, :, matrix] = part.reshape(slots, share, columns).astype(BF16)
        part_copies.append(pltpu.make_async_copy(part_buf.at[step], part_ref.at[step], part_sem.at[step]))
        part_copies[step].start()
    for copy in part_copies:
        copy.wait()


def hidden_layer(got, weights, slots):
    steps, _, units, columns = weights.shape
    rows = got.shape[0]
    total = rows // 16 * CAPACITY
    padded = -(-total // 128) * 128
    width = steps * columns
    far = pl.BlockSpec(memory_space=pltpu.MemorySpace.HBM)
    near = pl.BlockSpec(memory_space=pltpu.VMEM)
    part_shape = (steps, slots, 3, units // slots, columns)
    return pl.pallas_call(
        hidden_kernel,
        in_specs=[pl.BlockSpec(memory_space=pl.ANY), far],
        out_specs=[far, near, near, near, near],
        out_shape=[
            jax.ShapeDtypeStruct(part_shape, BF16),
            jax.ShapeDtypeStruct((total, units), BF16),
            jax.ShapeDtypeStruct((total, units), BF16),
            jax.ShapeDtypeStruct((total, units), BF16),
            jax.ShapeDtypeStruct((steps, total, columns), BF16),
        ],
        scratch_shapes=[
            pltpu.VMEM((steps, rows, columns), BF16),
            pltpu.VMEM((rows, width // 4), BF16),
            pltpu.VMEM(weights.shape, BF16),
            pltpu.VMEM(part_shape, BF16),
            pltpu.VMEM((steps, padded, columns), BF16),
            pltpu.VMEM((steps, padded, columns), BF16),
            pltpu.VMEM((total, units), F32),
            pltpu.VMEM((total, units), F32),
            pltpu.VMEM((total, units), F32),
            pltpu.VMEM((units, padded), BF16),
            pltpu.VMEM((units, padded), BF16),
            pltpu.VMEM((units, padded), BF16),
            pltpu.SemaphoreType.DMA((steps,)),
            pltpu.SemaphoreType.DMA,
            pltpu.SemaphoreType.DMA((steps,)),
            pltpu.SemaphoreType.DMA((steps,)),
        ],
        compiler_params=params(),
    )(got, weights)


def pair_kernel(gate_grad_ref, up_grad_ref, hidden_ref, scaled_ref, w_ref, out_ref, w_buf, w_sem):
    steps, _, units, columns = w_buf.shape
    mains = out_ref.shape[0]
    count = mains // MAIN
    rests = count * 2
    width = steps * columns
    per_quarter = width // 4 // columns
    copies = [pltpu.make_async_copy(w_ref.at[step], w_buf.at[step], w_sem.at[step]) for step in range(steps)]
    for copy in copies:
        copy.start()

    row, column = iota((mains, rests), 0), iota((mains, rests), 1)
    inner = row & 7
    rest_sums = [None] * per_quarter
    dots = None
    for step in range(steps):
        copies[step].wait()
        grad = matmul(gate_grad_ref[...], w_buf[step, 0]) + matmul(up_grad_ref[...], w_buf[step, 1])
        grad = grad.astype(BF16)
        out_ref[:, pl.ds(step * columns, columns)] = grad[:mains]
        placed = ones_where(((inner >> 1) == step // per_quarter) & (column == (row >> 3) * 2 + (inner & 1)))
        moved = matmul(placed, grad[mains:])
        which = step % per_quarter
        rest_sums[which] = moved if rest_sums[which] is None else rest_sums[which] + moved
        term = matmul(hidden_ref[...], w_buf[step, 2]) * scaled_ref[step].astype(F32)
        dots = term if dots is None else dots + term

    for which in range(per_quarter):
        out_ref[:, pl.ds(width + which * columns, columns)] = rest_sums[which].astype(BF16)
    dots = jnp.broadcast_to(jnp.sum(dots, axis=1, keepdims=True), (mains + rests, LANES)).astype(BF16)
    moved = matmul(ones_where((inner < 2) & (column == (row >> 3) * 2 + inner)), dots[mains:])
    lane = iota((mains, LANES), 1)
    out_ref[:, pl.ds(width + width // 4, LANES)] = jnp.where(
        lane < LANES // 2, dots[:mains].astype(F32), moved
    ).astype(BF16)


def pair_layer(gate_grad, up_grad, hidden, scaled, weights):
    steps, _, units, columns = weights.shape
    mains = gate_grad.shape[0] // CAPACITY * MAIN
    width = steps * columns
    near = pl.BlockSpec(memory_space=pltpu.VMEM)
    return pl.pallas_call(
        pair_kernel,
        in_specs=[near, near, near, near, pl.BlockSpec(memory_space=pltpu.MemorySpace.HBM)],
        out_specs=near,
        out_shape=jax.ShapeDtypeStruct((mains, width + width // 4 + LANES), BF16),
        scratch_shapes=[pltpu.VMEM(weights.shape, BF16), pltpu.SemaphoreType.DMA((steps,))],
        compiler_params=params(),
    )(gate_grad, up_grad, hidden, scaled, weights)


def combine_kernel(slots_ref, weights_ref, back_ref, token_ref, prob_ref):
    tokens, width = token_ref.shape
    mains = back_ref.shape[0]
    count = mains // MAIN
    quarter = width // 4
    first, second = slots_ref[:, 0:1], slots_ref[:, 1:2]
    column = iota((tokens, count), 1)
    in_first, in_second = first == column, second == column
    before = matmul(
        ones_where(iota((tokens, tokens), 0) > iota((tokens, tokens), 1)),
        ones_where(in_first | in_second),
    )
    rank_first = jnp.sum(jnp.where(in_first, before, 0.0), axis=1, keepdims=True).astype(I32)
    rank_second = jnp.sum(jnp.where(in_second, before, 0.0), axis=1, keepdims=True).astype(I32)
    code_first = first * 16 + rank_first
    code_second = second * 16 + rank_second

    cell = iota((tokens, mains), 1)
    code = (cell >> 3) * 16 + (cell & 7)
    main_first, main_second = code == code_first, code == code_second
    chosen = ones_where(main_first | main_second)
    code = (cell >> 3) * 16 + MAIN + (cell & 1)
    rest_hit = (code == code_first) | (code == code_second)
    rest_rows = back_ref[:, pl.ds(width, quarter)]
    for part in range(4):
        at = pl.ds(part * quarter, quarter)
        picked = ones_where(rest_hit & (((cell >> 1) & 3) == part))
        token_ref[:, at] = (matmul(chosen, back_ref[:, at]) + matmul(picked, rest_rows)).astype(BF16)

    probs = back_ref[:, pl.ds(width + quarter, LANES)]
    inner = cell & 7
    code = jnp.where(inner < 2, (cell >> 3) * 16 + MAIN + inner, -1)
    found = []
    for main_hit, mine in ((main_first, code_first), (main_second, code_second)):
        of_main = matmul(ones_where(main_hit), probs)[:, 0:1]
        of_rest = matmul(ones_where(code == mine), probs)[:, LANES // 2 : LANES // 2 + 1]
        found.append(of_main + of_rest)
    prob_ref[...] = (jnp.concatenate(found, axis=1) / weights_ref[...].astype(F32)).astype(BF16)


def combine(routed_slots, route_probs, back, tokens, width):
    return pl.pallas_call(
        combine_kernel,
        out_shape=[
            jax.ShapeDtypeStruct((tokens, width), BF16),
            jax.ShapeDtypeStruct((tokens, 2), BF16),
        ],
        compiler_params=params(),
    )(routed_slots, route_probs, back)


def fold_kernel(placement_ref, part_ref, gate_ref, up_ref, down_ref, total):
    total[...] = jnp.zeros_like(total)

    def one(slot, carry):
        expert = placement_ref[slot]
        total[expert] += part_ref[slot].astype(F32)
        return carry

    lax.fori_loop(0, part_ref.shape[0], one, 0)
    gate_ref[...] = total[:, 0].astype(BF16)
    up_ref[...] = total[:, 1].astype(BF16)
    down_ref[...] = total[:, 2].astype(BF16)


def fold(placement, parts, experts):
    slots, _, share, columns = parts.shape
    spec = pl.BlockSpec((experts, share, columns), lambda i, placement: (0, 0, 0))
    return pl.pallas_call(
        fold_kernel,
        grid_spec=pltpu.PrefetchScalarGridSpec(
            num_scalar_prefetch=1,
            grid=(1,),
            in_specs=[pl.BlockSpec((slots, 3, share, columns), lambda i, placement: (0, 0, 0, 0))],
            out_specs=[spec] * 3,
            scratch_shapes=[pltpu.VMEM((experts, 3, share, columns), F32)],
        ),
        out_shape=[jax.ShapeDtypeStruct((experts, share, columns), BF16)] * 3,
        compiler_params=params(),
    )(placement, parts)


def over_expert(value):
    return lax.all_to_all(value, "expert", split_axis=0, concat_axis=0, tiled=True)


def on_device(tokens, cotangent, routed_slots, route_probs, placement, w_gate, w_up, w_down):
    slots = lax.axis_size("expert")
    groups = lax.axis_size("dp")
    token_rows, width = tokens.shape
    columns = width // groups
    experts, share, _ = w_gate.shape
    hidden = share * slots

    index = jnp.concatenate([lax.axis_index("dp").astype(I32)[None], placement])
    wanted = pick(index, w_gate, w_up, w_down, slots, columns)
    payload = pack(routed_slots.T, route_probs.T.astype(F32), tokens, cotangent, slots)
    mine = over_expert(wanted)
    mine, payload = lax.optimization_barrier((mine, payload))
    mine = mine.transpose(1, 0, 2, 3).reshape(3, hidden, columns)
    weights = lax.all_gather(mine, "dp", axis=0)
    got = over_expert(payload.reshape(slots, 2 * MAIN, -1)).reshape(payload.shape)

    parts, gate_grad, up_grad, hidden_rows, scaled = hidden_layer(got, weights, slots)
    summed = lax.psum_scatter(parts, "dp", scatter_dimension=0)
    pairs = pair_layer(gate_grad, up_grad, hidden_rows, scaled, weights)
    back = over_expert(pairs.reshape(slots, MAIN, -1)).reshape(pairs.shape)
    token_grad, prob_grad = combine(routed_slots, route_probs, back, token_rows, width)

    grads = fold(placement, over_expert(summed), experts)
    return (token_grad, prob_grad, *grads)


def solution(mesh):
    placed = (
        P(("dp", "expert"), None),
        P(("dp", "expert"), None),
        P(("dp", "expert"), None),
        P(("dp", "expert"), None),
        P(),
        P(None, "expert", None),
        P(None, "expert", None),
        P(None, "expert", None),
    )
    return jax.shard_map(
        on_device,
        mesh=mesh,
        in_specs=placed,
        out_specs=(
            P(("dp", "expert"), None),
            P(("dp", "expert"), None),
            P(None, "expert", "dp"),
            P(None, "expert", "dp"),
            P(None, "expert", "dp"),
        ),
        check_vma=False,
    )
```

```python
import functools

import jax
import jax.numpy as jnp
from jax import lax
from jax.experimental import pallas as pl
from jax.experimental.pallas import tpu as pltpu
from jax.sharding import PartitionSpec as P

F32 = jnp.float32
BF16 = jnp.bfloat16
I32 = jnp.int32
CAPACITY = 10
MAIN = 8
LANES = 128


def params(mib=20):
    return pltpu.CompilerParams(vmem_limit_bytes=mib * 1024 * 1024)


def far():
    return pl.BlockSpec(memory_space=pltpu.MemorySpace.HBM)


def near():
    return pl.BlockSpec(memory_space=pltpu.VMEM)


def iota(shape, dim):
    return lax.broadcasted_iota(I32, shape, dim)


def ones_where(mask):
    return jnp.where(mask, 1.0, 0.0).astype(BF16)


def matmul(a, b):
    return jnp.dot(a, b, preferred_element_type=F32)


def matmul_t(a, b):
    return lax.dot_general(a, b, (((1,), (1,)), ((), ())), preferred_element_type=F32)


def matmul_tt(a, b):
    return lax.dot_general(a, b, (((0,), (1,)), ((), ())), preferred_element_type=F32)


def pick_kernel(placement_ref, gate_ref, up_ref, down_ref, out_ref, buf, sem):
    columns = out_ref.shape[3]
    at = pl.ds(pl.multiple_of(lax.axis_index("dp") * columns, columns), columns)
    copies = [
        pltpu.make_async_copy(ref.at[:, :, at], buf.at[matrix], sem.at[matrix])
        for matrix, ref in enumerate((gate_ref, up_ref, down_ref))
    ]
    for copy in copies:
        copy.start()
    for matrix, copy in enumerate(copies):
        copy.wait()
        for slot in range(out_ref.shape[0]):
            out_ref[slot, matrix] = buf[matrix, placement_ref[slot]]


def pick(placement, w_gate, w_up, w_down, slots, columns):
    experts, share, _ = w_gate.shape
    return pl.pallas_call(
        pick_kernel,
        in_specs=[pl.BlockSpec(memory_space=pltpu.SMEM), far(), far(), far()],
        out_specs=near(),
        out_shape=jax.ShapeDtypeStruct((slots, 3, share, columns), BF16),
        scratch_shapes=[pltpu.VMEM((3, experts, share, columns), BF16), pltpu.SemaphoreType.DMA((3,))],
        compiler_params=params(56),
    )(placement, w_gate, w_up, w_down)


def whole(block):
    slots, share, columns = block.shape
    return block.reshape(slots * share, columns)


def pack_kernel(slots_ref, probs_ref, tok_ref, cot_ref, out_ref):
    tokens, width = tok_ref.shape
    count = out_ref.shape[0] // (2 * MAIN)
    quarter = width // 4
    first, second = slots_ref[0:1, :], slots_ref[1:2, :]
    row = iota((count, tokens), 0)
    in_first, in_second = first == row, second == row
    before = matmul(
        ones_where(in_first | in_second),
        ones_where(iota((tokens, tokens), 0) < iota((tokens, tokens), 1)),
    )
    rank_first = jnp.sum(jnp.where(in_first, before, 0.0), axis=0, keepdims=True).astype(I32)
    rank_second = jnp.sum(jnp.where(in_second, before, 0.0), axis=0, keepdims=True).astype(I32)
    code_first = first * 16 + rank_first
    code_second = second * 16 + rank_second

    def look_up(code):
        hit_first, hit_second = code == code_first, code == code_second
        weight = jnp.sum(
            jnp.where(hit_first, probs_ref[0:1, :], 0.0) + jnp.where(hit_second, probs_ref[1:2, :], 0.0),
            axis=1,
            keepdims=True,
        )
        return hit_first | hit_second, weight

    row = iota((count * MAIN, tokens), 0)
    hit, weight = look_up((row >> 3) * 16 + (row & 7))
    chosen = ones_where(hit)
    for part in range(4):
        at = pl.ds(part * quarter, quarter)
        tok_rows = matmul(chosen, tok_ref[:, at]).reshape(count, MAIN, quarter)
        cot_rows = (weight * matmul(chosen, cot_ref[:, at])).reshape(count, MAIN, quarter)
        both = jnp.concatenate([tok_rows[:, None], cot_rows[:, None]], axis=1)
        out_ref[:, at] = both.reshape(count * 2 * MAIN, quarter).astype(BF16)

    row = iota((count * 2 * MAIN, tokens), 0)
    hit, weight = look_up((row >> 4) * 16 + MAIN + (row & 1))
    is_cot = ((row >> 1) & 1) == 1
    tok_rows = jnp.zeros((count * 2 * MAIN, quarter), F32)
    cot_rows = jnp.zeros((count * 2 * MAIN, quarter), F32)
    for part in range(4):
        here = hit & (((row >> 2) & 3) == part)
        at = pl.ds(part * quarter, quarter)
        tok_rows += matmul(ones_where(here & jnp.logical_not(is_cot)), tok_ref[:, at])
        cot_rows += matmul(ones_where(here & is_cot), cot_ref[:, at])
    out_ref[:, pl.ds(width, quarter)] = (tok_rows + weight * cot_rows).astype(BF16)


def pack(slots_t, probs_t, tokens, cotangent, slots):
    width = tokens.shape[1]
    return pl.pallas_call(
        pack_kernel,
        out_shape=jax.ShapeDtypeStruct((slots * 2 * MAIN, width + width // 4), BF16),
        compiler_params=params(),
    )(slots_t, probs_t, tokens, cotangent)


def hidden_kernel(
    got_ref, w_ref,
    part_ref, gate_grad_ref, up_grad_ref, hidden_ref, scaled_ref,
    got_buf, rest_buf, w_buf, part_buf, tok_keep, scaled_keep, gate_acc, up_acc, down_acc, gate_t, up_t, hidden_t,
    got_sem, rest_sem, w_sem, part_sem,
):
    quarters, rows, quarter = got_buf.shape
    steps, slots, _, share, columns = w_buf.shape
    units = slots * share
    each = steps // quarters
    count = rows // 16
    mains, rests = count * MAIN, count * 2
    total = mains + rests
    padded = tok_keep.shape[1]

    def got_copy(part):
        at = pl.ds(pl.multiple_of(part * quarter, quarter), quarter)
        return pltpu.make_async_copy(got_ref.at[:, at], got_buf.at[part], got_sem.at[part])

    def w_copy(part):
        at = pl.ds(part * each, each)
        return pltpu.make_async_copy(w_ref.at[at], w_buf.at[at], w_sem.at[part])

    rest_copy = pltpu.make_async_copy(got_ref.at[:, pl.ds(quarters * quarter, quarter)], rest_buf, rest_sem)
    rest_copy.start()
    for part in range(2):
        got_copy(part).start()
        w_copy(part).start()
    gate_acc[...] = jnp.zeros_like(gate_acc)
    up_acc[...] = jnp.zeros_like(up_acc)
    down_acc[...] = jnp.zeros_like(down_acc)
    for step in range(steps):
        tok_keep[step, total:padded] = jnp.zeros((padded - total, columns), BF16)
        scaled_keep[step, total:padded] = jnp.zeros((padded - total, columns), BF16)
    row, column = iota((2 * rests, rows), 0), iota((2 * rests, rows), 1)
    second = jnp.where(row >= rests, 1, 0)
    inner = row - second * rests
    offset = column - (inner >> 1) * 16 - second * 2 - (inner & 1)
    rest_copy.wait()

    def forward(part, carry):
        @pl.when(part + 2 < quarters)
        def _():
            got_copy(part + 2).start()
            w_copy(part + 2).start()

        got_copy(part).wait()
        block = got_buf[part].astype(F32).reshape(count, 2, MAIN, quarter)
        rest = matmul(ones_where(offset == part * 4), rest_buf[...])
        tok = jnp.concatenate([block[:, 0].reshape(mains, quarter), rest[:rests]], axis=0).astype(BF16)
        scaled = jnp.concatenate([block[:, 1].reshape(mains, quarter), rest[rests:]], axis=0).astype(BF16)
        for i in range(each):
            at = slice(i * columns, (i + 1) * columns)
            tok_keep[part * each + i, 0:total] = tok[:, at]
            scaled_keep[part * each + i, 0:total] = scaled[:, at]
            scaled_ref[part * each + i] = scaled[:, at]
        w_copy(part).wait()
        for acc, left, matrix in ((gate_acc, tok, 0), (up_acc, tok, 1), (down_acc, scaled, 2)):
            right = jnp.concatenate([whole(w_buf[part * each + i, :, matrix]) for i in range(each)], axis=1)
            acc[...] += matmul_t(left, right)
        return carry

    lax.fori_loop(0, quarters, forward, 0)

    for start in range(0, padded, 128):
        size = min(128, total - start)
        at = pl.ds(start, size)
        gate_pre, up_pre, hidden_grad = gate_acc[at, :], up_acc[at, :], down_acc[at, :]
        sigma = jax.nn.sigmoid(gate_pre)
        swish = gate_pre * sigma
        hidden = swish * up_pre
        gate_grad = hidden_grad * up_pre * sigma * (1.0 + gate_pre * (1.0 - sigma))
        up_grad = hidden_grad * swish
        for value, out, out_t in (
            (hidden, hidden_ref, hidden_t),
            (gate_grad, gate_grad_ref, gate_t),
            (up_grad, up_grad_ref, up_t),
        ):
            out[at, :] = value.astype(BF16)
            if size < 128:
                value = jnp.concatenate([value, jnp.zeros((128 - size, units), F32)], axis=0)
            out_t[:, pl.ds(start, 128)] = value.T.astype(BF16)

    def part_copy(step):
        return pltpu.make_async_copy(part_buf.at[step], part_ref.at[step], part_sem.at[step])

    def backward(step):
        for matrix, (left, right) in enumerate(((gate_t, tok_keep), (up_t, tok_keep), (hidden_t, scaled_keep))):
            part = matmul(left[...], right[step])
            part_buf[step, :, matrix] = part.reshape(slots, share, columns).astype(BF16)
        part_copy(step).start()

    for step in range(steps):
        backward(step)
    for step in range(steps):
        part_copy(step).wait()


def hidden_layer(got, weights):
    steps, slots, _, share, columns = weights.shape
    units = slots * share
    rows = got.shape[0]
    total = rows // 16 * CAPACITY
    padded = -(-total // 128) * 128
    quarter = steps * columns // 4
    return pl.pallas_call(
        hidden_kernel,
        in_specs=[far(), far()],
        out_specs=[far(), near(), near(), near(), near()],
        out_shape=[
            jax.ShapeDtypeStruct(weights.shape, BF16),
            jax.ShapeDtypeStruct((total, units), BF16),
            jax.ShapeDtypeStruct((total, units), BF16),
            jax.ShapeDtypeStruct((total, units), BF16),
            jax.ShapeDtypeStruct((steps, total, columns), BF16),
        ],
        scratch_shapes=[
            pltpu.VMEM((4, rows, quarter), BF16),
            pltpu.VMEM((rows, quarter), BF16),
            pltpu.VMEM(weights.shape, BF16),
            pltpu.VMEM(weights.shape, BF16),
            pltpu.VMEM((steps, padded, columns), BF16),
            pltpu.VMEM((steps, padded, columns), BF16),
            pltpu.VMEM((total, units), F32),
            pltpu.VMEM((total, units), F32),
            pltpu.VMEM((total, units), F32),
            pltpu.VMEM((units, padded), BF16),
            pltpu.VMEM((units, padded), BF16),
            pltpu.VMEM((units, padded), BF16),
            pltpu.SemaphoreType.DMA((4,)),
            pltpu.SemaphoreType.DMA,
            pltpu.SemaphoreType.DMA((4,)),
            pltpu.SemaphoreType.DMA((steps,)),
        ],
        compiler_params=params(56),
    )(got, weights)


def pair_kernel(
    gate_grad_ref, up_grad_ref, hidden_ref, scaled_ref, w_ref, out_ref, w_buf, rest_acc, dot_acc, w_sem
):
    steps, _, _, _, columns = w_buf.shape
    mains = out_ref.shape[0]
    count = mains // MAIN
    rests = count * 2
    width = steps * columns
    per_quarter = width // 4 // columns

    def w_copy(step):
        return pltpu.make_async_copy(w_ref.at[step], w_buf.at[step], w_sem.at[step])

    for step in range(3):
        w_copy(step).start()
    rest_acc[...] = jnp.zeros_like(rest_acc)
    dot_acc[...] = jnp.zeros_like(dot_acc)
    row, column = iota((mains, rests), 0), iota((mains, rests), 1)
    inner = row & 7
    in_place = column == (row >> 3) * 2 + (inner & 1)

    def one(step):
        if step + 3 < steps:
            w_copy(step + 3).start()
        w_copy(step).wait()
        grad = matmul(gate_grad_ref[...], whole(w_buf[step, :, 0]))
        grad += matmul(up_grad_ref[...], whole(w_buf[step, :, 1]))
        grad = grad.astype(BF16)
        out_ref[:, pl.ds(step * columns, columns)] = grad[:mains]
        placed = ones_where(in_place & ((inner >> 1) == step // per_quarter))
        rest_acc[step % per_quarter] += matmul(placed, grad[mains:])
        dot_acc[...] += matmul(hidden_ref[...], whole(w_buf[step, :, 2])) * scaled_ref[step].astype(F32)

    for step in range(steps):
        one(step)
    for which in range(per_quarter):
        out_ref[:, pl.ds(width + which * columns, columns)] = rest_acc[which].astype(BF16)
    dots = jnp.sum(dot_acc[...], axis=1, keepdims=True)
    dots = jnp.broadcast_to(dots, (mains + rests, LANES)).astype(BF16)
    moved = matmul(ones_where((inner < 2) & (column == (row >> 3) * 2 + inner)), dots[mains:])
    lane = iota((mains, LANES), 1)
    out_ref[:, pl.ds(width + width // 4, LANES)] = jnp.where(
        lane < LANES // 2, dots[:mains].astype(F32), moved
    ).astype(BF16)


def pair_layer(gate_grad, up_grad, hidden, scaled, weights):
    steps, _, _, _, columns = weights.shape
    total = gate_grad.shape[0]
    mains = total // CAPACITY * MAIN
    width = steps * columns
    return pl.pallas_call(
        pair_kernel,
        in_specs=[near(), near(), near(), near(), far()],
        out_specs=near(),
        out_shape=jax.ShapeDtypeStruct((mains, width + width // 4 + LANES), BF16),
        scratch_shapes=[
            pltpu.VMEM(weights.shape, BF16),
            pltpu.VMEM((width // 4 // columns, mains, columns), F32),
            pltpu.VMEM((total, columns), F32),
            pltpu.SemaphoreType.DMA((steps,)),
        ],
        compiler_params=params(56),
    )(gate_grad, up_grad, hidden, scaled, weights)


def combine_kernel(slots_ref, weights_ref, back_ref, token_ref, prob_ref):
    tokens, width = token_ref.shape
    mains = back_ref.shape[0]
    count = mains // MAIN
    quarter = width // 4
    first, second = slots_ref[:, 0:1], slots_ref[:, 1:2]
    column = iota((tokens, count), 1)
    in_first, in_second = first == column, second == column
    before = matmul(
        ones_where(iota((tokens, tokens), 0) > iota((tokens, tokens), 1)),
        ones_where(in_first | in_second),
    )
    rank_first = jnp.sum(jnp.where(in_first, before, 0.0), axis=1, keepdims=True).astype(I32)
    rank_second = jnp.sum(jnp.where(in_second, before, 0.0), axis=1, keepdims=True).astype(I32)
    code_first = first * 16 + rank_first
    code_second = second * 16 + rank_second

    cell = iota((tokens, mains), 1)
    code = (cell >> 3) * 16 + (cell & 7)
    main_first, main_second = code == code_first, code == code_second
    chosen = ones_where(main_first | main_second)
    code = (cell >> 3) * 16 + MAIN + (cell & 1)
    rest_hit = (code == code_first) | (code == code_second)
    rest_rows = back_ref[:, pl.ds(width, quarter)]
    for part in range(4):
        at = pl.ds(part * quarter, quarter)
        picked = ones_where(rest_hit & (((cell >> 1) & 3) == part))
        token_ref[:, at] = (matmul(chosen, back_ref[:, at]) + matmul(picked, rest_rows)).astype(BF16)

    probs = back_ref[:, pl.ds(width + quarter, LANES)]
    inner = cell & 7
    code = jnp.where(inner < 2, (cell >> 3) * 16 + MAIN + inner, -1)
    found = []
    for main_hit, mine in ((main_first, code_first), (main_second, code_second)):
        of_main = matmul_tt(probs, ones_where(main_hit))[0:1, :]
        of_rest = matmul_tt(probs, ones_where(code == mine))[LANES // 2 : LANES // 2 + 1, :]
        found.append(of_main + of_rest)
    prob_ref[...] = (jnp.concatenate(found, axis=0) / weights_ref[...].astype(F32)).astype(BF16)


def combine(routed_slots, probs_t, back, tokens, width):
    return pl.pallas_call(
        combine_kernel,
        out_shape=[
            jax.ShapeDtypeStruct((tokens, width), BF16),
            jax.ShapeDtypeStruct((2, tokens), BF16),
        ],
        compiler_params=params(),
    )(routed_slots, probs_t, back)


def fold_kernel(placement_ref, part_ref, gate_ref, up_ref, down_ref, total):
    total[...] = jnp.zeros_like(total)

    def one(slot, carry):
        expert = placement_ref[slot]
        total[expert] += part_ref[slot].astype(F32)
        return carry

    lax.fori_loop(0, part_ref.shape[0], one, 0)
    gate_ref[...] = total[:, 0].astype(BF16)
    up_ref[...] = total[:, 1].astype(BF16)
    down_ref[...] = total[:, 2].astype(BF16)


def fold(placement, parts, experts):
    slots, _, share, columns = parts.shape
    spec = pl.BlockSpec((experts, share, columns), lambda i, placement: (0, 0, 0))
    return pl.pallas_call(
        fold_kernel,
        grid_spec=pltpu.PrefetchScalarGridSpec(
            num_scalar_prefetch=1,
            grid=(1,),
            in_specs=[pl.BlockSpec((slots, 3, share, columns), lambda i, placement: (0, 0, 0, 0))],
            out_specs=[spec] * 3,
            scratch_shapes=[pltpu.VMEM((experts, 3, share, columns), F32)],
        ),
        out_shape=[jax.ShapeDtypeStruct((experts, share, columns), BF16)] * 3,
        compiler_params=params(),
    )(placement, parts)


def over_expert(value):
    return lax.all_to_all(value, "expert", split_axis=0, concat_axis=0, tiled=True)


def on_device(tokens, cotangent, routed_slots, route_probs, placement, w_gate, w_up, w_down):
    slots = lax.axis_size("expert")
    groups = lax.axis_size("dp")
    token_rows, width = tokens.shape
    columns = width // groups
    experts, share, _ = w_gate.shape

    wanted = pick(placement, w_gate, w_up, w_down, slots, columns)
    payload = pack(routed_slots.T, route_probs.T.astype(F32), tokens, cotangent, slots)
    mine = over_expert(wanted)
    mine, payload = lax.optimization_barrier((mine, payload))
    weights = lax.all_gather(mine, "dp", axis=0)
    got = over_expert(payload.reshape(slots, 2 * MAIN, -1)).reshape(payload.shape)

    parts, gate_grad, up_grad, hidden_rows, scaled = hidden_layer(got, weights)
    summed = lax.psum_scatter(parts, "dp", scatter_dimension=0)
    pairs = pair_layer(gate_grad, up_grad, hidden_rows, scaled, weights)
    back = over_expert(pairs.reshape(slots, MAIN, -1)).reshape(pairs.shape)
    token_grad, prob_grad = combine(routed_slots, route_probs.T, back, token_rows, width)

    summed, token_grad, prob_grad = lax.optimization_barrier((summed, token_grad, prob_grad))
    grads = fold(placement, over_expert(summed), experts)
    return (token_grad, prob_grad.T, *grads)


def solution(mesh):
    placed = (
        P(("dp", "expert"), None),
        P(("dp", "expert"), None),
        P(("dp", "expert"), None),
        P(("dp", "expert"), None),
        P(),
        P(None, "expert", None),
        P(None, "expert", None),
        P(None, "expert", None),
    )
    return jax.shard_map(
        on_device,
        mesh=mesh,
        in_specs=placed,
        out_specs=(
            P(("dp", "expert"), None),
            P(("dp", "expert"), None),
            P(None, "expert", "dp"),
            P(None, "expert", "dp"),
            P(None, "expert", "dp"),
        ),
        check_vma=False,
    )
```

```python
import functools

import jax
import jax.numpy as jnp
from jax import lax
from jax.experimental import pallas as pl
from jax.experimental.pallas import tpu as pltpu
from jax.sharding import PartitionSpec as P

F32 = jnp.float32
BF16 = jnp.bfloat16
I32 = jnp.int32
CAPACITY = 10
MAIN = 8
LANES = 128


def params(mib=20):
    return pltpu.CompilerParams(vmem_limit_bytes=mib * 1024 * 1024)


def far():
    return pl.BlockSpec(memory_space=pltpu.MemorySpace.HBM)


def near():
    return pl.BlockSpec(memory_space=pltpu.VMEM)


def iota(shape, dim):
    return lax.broadcasted_iota(I32, shape, dim)


def ones_where(mask):
    return jnp.where(mask, 1.0, 0.0).astype(BF16)


def matmul(a, b):
    return jnp.dot(a, b, preferred_element_type=F32)


def matmul_t(a, b):
    return lax.dot_general(a, b, (((1,), (1,)), ((), ())), preferred_element_type=F32)


def matmul_tt(a, b):
    return lax.dot_general(a, b, (((0,), (1,)), ((), ())), preferred_element_type=F32)


def pick_kernel(placement_ref, gate_ref, up_ref, down_ref, out_ref, buf, sem):
    columns = out_ref.shape[3]
    at = pl.ds(pl.multiple_of(lax.axis_index("dp") * columns, columns), columns)
    copies = [
        pltpu.make_async_copy(ref.at[:, :, at], buf.at[matrix], sem.at[matrix])
        for matrix, ref in enumerate((gate_ref, up_ref, down_ref))
    ]
    for copy in copies:
        copy.start()
    for matrix, copy in enumerate(copies):
        copy.wait()
        for slot in range(out_ref.shape[0]):
            out_ref[slot, matrix] = buf[matrix, placement_ref[slot]]


def pick(placement, w_gate, w_up, w_down, slots, columns):
    experts, share, _ = w_gate.shape
    return pl.pallas_call(
        pick_kernel,
        in_specs=[pl.BlockSpec(memory_space=pltpu.SMEM), far(), far(), far()],
        out_specs=near(),
        out_shape=jax.ShapeDtypeStruct((slots, 3, share, columns), BF16),
        scratch_shapes=[pltpu.VMEM((3, experts, share, columns), BF16), pltpu.SemaphoreType.DMA((3,))],
        compiler_params=params(56),
    )(placement, w_gate, w_up, w_down)


def whole(block):
    slots, share, columns = block.shape
    return block.reshape(slots * share, columns)


def pack_kernel(slots_ref, probs_ref, tok_ref, cot_ref, out_ref):
    tokens, width = tok_ref.shape
    count = out_ref.shape[0] // (2 * MAIN)
    quarter = width // 4
    first, second = slots_ref[0:1, :], slots_ref[1:2, :]
    row = iota((count, tokens), 0)
    in_first, in_second = first == row, second == row
    before = matmul(
        ones_where(in_first | in_second),
        ones_where(iota((tokens, tokens), 0) < iota((tokens, tokens), 1)),
    )
    rank_first = jnp.sum(jnp.where(in_first, before, 0.0), axis=0, keepdims=True).astype(I32)
    rank_second = jnp.sum(jnp.where(in_second, before, 0.0), axis=0, keepdims=True).astype(I32)
    code_first = first * 16 + rank_first
    code_second = second * 16 + rank_second

    def look_up(code):
        hit_first, hit_second = code == code_first, code == code_second
        weight = jnp.sum(
            jnp.where(hit_first, probs_ref[0:1, :], 0.0) + jnp.where(hit_second, probs_ref[1:2, :], 0.0),
            axis=1,
            keepdims=True,
        )
        return hit_first | hit_second, weight

    row = iota((count * MAIN, tokens), 0)
    hit, weight = look_up((row >> 3) * 16 + (row & 7))
    chosen = ones_where(hit)
    for part in range(4):
        at = pl.ds(part * quarter, quarter)
        tok_rows = matmul(chosen, tok_ref[:, at]).reshape(count, MAIN, quarter)
        cot_rows = (weight * matmul(chosen, cot_ref[:, at])).reshape(count, MAIN, quarter)
        both = jnp.concatenate([tok_rows[:, None], cot_rows[:, None]], axis=1)
        out_ref[:, at] = both.reshape(count * 2 * MAIN, quarter).astype(BF16)

    row = iota((count * 2 * MAIN, tokens), 0)
    hit, weight = look_up((row >> 4) * 16 + MAIN + (row & 1))
    is_cot = ((row >> 1) & 1) == 1
    tok_rows = jnp.zeros((count * 2 * MAIN, quarter), F32)
    cot_rows = jnp.zeros((count * 2 * MAIN, quarter), F32)
    for part in range(4):
        here = hit & (((row >> 2) & 3) == part)
        at = pl.ds(part * quarter, quarter)
        tok_rows += matmul(ones_where(here & jnp.logical_not(is_cot)), tok_ref[:, at])
        cot_rows += matmul(ones_where(here & is_cot), cot_ref[:, at])
    out_ref[:, pl.ds(width, quarter)] = (tok_rows + weight * cot_rows).astype(BF16)


def pack(slots_t, probs_t, tokens, cotangent, slots):
    width = tokens.shape[1]
    return pl.pallas_call(
        pack_kernel,
        out_shape=jax.ShapeDtypeStruct((slots * 2 * MAIN, width + width // 4), BF16),
        compiler_params=params(),
    )(slots_t, probs_t, tokens, cotangent)


def hidden_kernel(
    got_ref, w_ref,
    part_ref, gate_grad_ref, up_grad_ref, hidden_ref, scaled_ref,
    got_buf, rest_buf, w_buf, part_buf, tok_keep, scaled_keep, gate_acc, up_acc, down_acc, gate_t, up_t, hidden_t,
    grad_keep, scaled_out, got_sem, rest_sem, w_sem, part_sem, grad_sem, scaled_sem,
):
    quarters, rows, quarter = got_buf.shape
    steps, slots, _, share, columns = w_buf.shape
    units = slots * share
    each = steps // quarters
    count = rows // 16
    mains, rests = count * MAIN, count * 2
    total = mains + rests
    padded = tok_keep.shape[1]

    def got_copy(part):
        at = pl.ds(pl.multiple_of(part * quarter, quarter), quarter)
        return pltpu.make_async_copy(got_ref.at[:, at], got_buf.at[part], got_sem.at[part])

    def w_copy(part):
        at = pl.ds(part * each, each)
        return pltpu.make_async_copy(w_ref.at[at], w_buf.at[at], w_sem.at[part])

    def scaled_copy(part):
        at = pl.ds(part * each, each)
        return pltpu.make_async_copy(scaled_out.at[at], scaled_ref.at[at], scaled_sem.at[part])

    rest_copy = pltpu.make_async_copy(got_ref.at[:, pl.ds(quarters * quarter, quarter)], rest_buf, rest_sem)
    rest_copy.start()
    for part in range(2):
        got_copy(part).start()
        w_copy(part).start()
    gate_acc[...] = jnp.zeros_like(gate_acc)
    up_acc[...] = jnp.zeros_like(up_acc)
    down_acc[...] = jnp.zeros_like(down_acc)
    for step in range(steps):
        tok_keep[step, total:padded] = jnp.zeros((padded - total, columns), BF16)
        scaled_keep[step, total:padded] = jnp.zeros((padded - total, columns), BF16)
    row, column = iota((2 * rests, rows), 0), iota((2 * rests, rows), 1)
    second = jnp.where(row >= rests, 1, 0)
    inner = row - second * rests
    offset = column - (inner >> 1) * 16 - second * 2 - (inner & 1)
    rest_copy.wait()

    def forward(part, carry):
        @pl.when(part + 2 < quarters)
        def _():
            got_copy(part + 2).start()
            w_copy(part + 2).start()

        got_copy(part).wait()
        block = got_buf[part].astype(F32).reshape(count, 2, MAIN, quarter)
        rest = matmul(ones_where(offset == part * 4), rest_buf[...])
        tok = jnp.concatenate([block[:, 0].reshape(mains, quarter), rest[:rests]], axis=0).astype(BF16)
        scaled = jnp.concatenate([block[:, 1].reshape(mains, quarter), rest[rests:]], axis=0).astype(BF16)
        for i in range(each):
            at = slice(i * columns, (i + 1) * columns)
            tok_keep[part * each + i, 0:total] = tok[:, at]
            scaled_keep[part * each + i, 0:total] = scaled[:, at]
            scaled_out[part * each + i] = scaled[:, at]
        scaled_copy(part).start()
        w_copy(part).wait()
        for acc, left, matrix in ((gate_acc, tok, 0), (up_acc, tok, 1), (down_acc, scaled, 2)):
            right = jnp.concatenate([whole(w_buf[part * each + i, :, matrix]) for i in range(each)], axis=1)
            acc[...] += matmul_t(left, right)
        return carry

    lax.fori_loop(0, quarters, forward, 0)

    for start in range(0, padded, 128):
        size = min(128, total - start)
        at = pl.ds(start, size)
        gate_pre, up_pre, hidden_grad = gate_acc[at, :], up_acc[at, :], down_acc[at, :]
        sigma = jax.nn.sigmoid(gate_pre)
        swish = gate_pre * sigma
        hidden = swish * up_pre
        gate_grad = hidden_grad * up_pre * sigma * (1.0 + gate_pre * (1.0 - sigma))
        up_grad = hidden_grad * swish
        for which, (value, out_t) in enumerate(((gate_grad, gate_t), (up_grad, up_t), (hidden, hidden_t))):
            grad_keep[which, at, :] = value.astype(BF16)
            if size < 128:
                value = jnp.concatenate([value, jnp.zeros((128 - size, units), F32)], axis=0)
            out_t[:, pl.ds(start, 128)] = value.T.astype(BF16)

    grad_copies = [
        pltpu.make_async_copy(grad_keep.at[which], out, grad_sem.at[which])
        for which, out in enumerate((gate_grad_ref, up_grad_ref, hidden_ref))
    ]
    for copy in grad_copies:
        copy.start()

    def part_copy(step):
        return pltpu.make_async_copy(part_buf.at[step], part_ref.at[step], part_sem.at[step])

    def backward(step):
        for matrix, (left, right) in enumerate(((gate_t, tok_keep), (up_t, tok_keep), (hidden_t, scaled_keep))):
            part = matmul(left[...], right[step])
            part_buf[step, :, matrix] = part.reshape(slots, share, columns).astype(BF16)
        part_copy(step).start()

    for step in range(steps):
        backward(step)
    for part in range(quarters):
        scaled_copy(part).wait()
    for copy in grad_copies:
        copy.wait()
    for step in range(steps):
        part_copy(step).wait()


def hidden_layer(got, weights):
    steps, slots, _, share, columns = weights.shape
    units = slots * share
    rows = got.shape[0]
    total = rows // 16 * CAPACITY
    padded = -(-total // 128) * 128
    quarter = steps * columns // 4
    return pl.pallas_call(
        hidden_kernel,
        in_specs=[far(), far()],
        out_specs=[far()] * 5,
        out_shape=[
            jax.ShapeDtypeStruct(weights.shape, BF16),
            jax.ShapeDtypeStruct((total, units), BF16),
            jax.ShapeDtypeStruct((total, units), BF16),
            jax.ShapeDtypeStruct((total, units), BF16),
            jax.ShapeDtypeStruct((steps, total, columns), BF16),
        ],
        scratch_shapes=[
            pltpu.VMEM((4, rows, quarter), BF16),
            pltpu.VMEM((rows, quarter), BF16),
            pltpu.VMEM(weights.shape, BF16),
            pltpu.VMEM(weights.shape, BF16),
            pltpu.VMEM((steps, padded, columns), BF16),
            pltpu.VMEM((steps, padded, columns), BF16),
            pltpu.VMEM((total, units), F32),
            pltpu.VMEM((total, units), F32),
            pltpu.VMEM((total, units), F32),
            pltpu.VMEM((units, padded), BF16),
            pltpu.VMEM((units, padded), BF16),
            pltpu.VMEM((units, padded), BF16),
            pltpu.VMEM((3, total, units), BF16),
            pltpu.VMEM((steps, total, columns), BF16),
            pltpu.SemaphoreType.DMA((4,)),
            pltpu.SemaphoreType.DMA,
            pltpu.SemaphoreType.DMA((4,)),
            pltpu.SemaphoreType.DMA((steps,)),
            pltpu.SemaphoreType.DMA((3,)),
            pltpu.SemaphoreType.DMA((4,)),
        ],
        compiler_params=params(56),
    )(got, weights)


def pair_kernel(
    gate_grad_ref, up_grad_ref, hidden_ref, scaled_ref, w_ref, out_ref, w_buf, rest_acc, dot_acc, w_sem
):
    steps, _, _, _, columns = w_buf.shape
    mains = out_ref.shape[0]
    count = mains // MAIN
    rests = count * 2
    width = steps * columns
    per_quarter = width // 4 // columns

    def w_copy(step):
        return pltpu.make_async_copy(w_ref.at[step], w_buf.at[step], w_sem.at[step])

    for step in range(3):
        w_copy(step).start()
    rest_acc[...] = jnp.zeros_like(rest_acc)
    dot_acc[...] = jnp.zeros_like(dot_acc)
    row, column = iota((mains, rests), 0), iota((mains, rests), 1)
    inner = row & 7
    in_place = column == (row >> 3) * 2 + (inner & 1)

    def one(step):
        if step + 3 < steps:
            w_copy(step + 3).start()
        w_copy(step).wait()
        grad = matmul(gate_grad_ref[...], whole(w_buf[step, :, 0]))
        grad += matmul(up_grad_ref[...], whole(w_buf[step, :, 1]))
        grad = grad.astype(BF16)
        out_ref[:, pl.ds(step * columns, columns)] = grad[:mains]
        placed = ones_where(in_place & ((inner >> 1) == step // per_quarter))
        rest_acc[step % per_quarter] += matmul(placed, grad[mains:])
        dot_acc[...] += matmul(hidden_ref[...], whole(w_buf[step, :, 2])) * scaled_ref[step].astype(F32)

    for step in range(steps):
        one(step)
    for which in range(per_quarter):
        out_ref[:, pl.ds(width + which * columns, columns)] = rest_acc[which].astype(BF16)
    dots = jnp.sum(dot_acc[...], axis=1, keepdims=True)
    dots = jnp.broadcast_to(dots, (mains + rests, LANES)).astype(BF16)
    moved = matmul(ones_where((inner < 2) & (column == (row >> 3) * 2 + inner)), dots[mains:])
    lane = iota((mains, LANES), 1)
    out_ref[:, pl.ds(width + width // 4, LANES)] = jnp.where(
        lane < LANES // 2, dots[:mains].astype(F32), moved
    ).astype(BF16)


def pair_layer(gate_grad, up_grad, hidden, scaled, weights):
    steps, _, _, _, columns = weights.shape
    total = gate_grad.shape[0]
    mains = total // CAPACITY * MAIN
    width = steps * columns
    return pl.pallas_call(
        pair_kernel,
        in_specs=[near(), near(), near(), near(), far()],
        out_specs=near(),
        out_shape=jax.ShapeDtypeStruct((mains, width + width // 4 + LANES), BF16),
        scratch_shapes=[
            pltpu.VMEM(weights.shape, BF16),
            pltpu.VMEM((width // 4 // columns, mains, columns), F32),
            pltpu.VMEM((total, columns), F32),
            pltpu.SemaphoreType.DMA((steps,)),
        ],
        compiler_params=params(56),
    )(gate_grad, up_grad, hidden, scaled, weights)


def combine_kernel(slots_ref, weights_ref, back_ref, token_ref, prob_ref):
    tokens, width = token_ref.shape
    mains = back_ref.shape[0]
    count = mains // MAIN
    quarter = width // 4
    first, second = slots_ref[:, 0:1], slots_ref[:, 1:2]
    column = iota((tokens, count), 1)
    in_first, in_second = first == column, second == column
    before = matmul(
        ones_where(iota((tokens, tokens), 0) > iota((tokens, tokens), 1)),
        ones_where(in_first | in_second),
    )
    rank_first = jnp.sum(jnp.where(in_first, before, 0.0), axis=1, keepdims=True).astype(I32)
    rank_second = jnp.sum(jnp.where(in_second, before, 0.0), axis=1, keepdims=True).astype(I32)
    code_first = first * 16 + rank_first
    code_second = second * 16 + rank_second

    cell = iota((tokens, mains), 1)
    code = (cell >> 3) * 16 + (cell & 7)
    main_first, main_second = code == code_first, code == code_second
    chosen = ones_where(main_first | main_second)
    code = (cell >> 3) * 16 + MAIN + (cell & 1)
    rest_hit = (code == code_first) | (code == code_second)
    rest_rows = back_ref[:, pl.ds(width, quarter)]
    for part in range(4):
        at = pl.ds(part * quarter, quarter)
        picked = ones_where(rest_hit & (((cell >> 1) & 3) == part))
        token_ref[:, at] = (matmul(chosen, back_ref[:, at]) + matmul(picked, rest_rows)).astype(BF16)

    probs = back_ref[:, pl.ds(width + quarter, LANES)]
    inner = cell & 7
    code = jnp.where(inner < 2, (cell >> 3) * 16 + MAIN + inner, -1)
    found = []
    for main_hit, mine in ((main_first, code_first), (main_second, code_second)):
        of_main = matmul_tt(probs, ones_where(main_hit))[0:1, :]
        of_rest = matmul_tt(probs, ones_where(code == mine))[LANES // 2 : LANES // 2 + 1, :]
        found.append(of_main + of_rest)
    prob_ref[...] = (jnp.concatenate(found, axis=0) / weights_ref[...].astype(F32)).astype(BF16)


def combine(routed_slots, probs_t, back, tokens, width):
    return pl.pallas_call(
        combine_kernel,
        out_shape=[
            jax.ShapeDtypeStruct((tokens, width), BF16),
            jax.ShapeDtypeStruct((2, tokens), BF16),
        ],
        compiler_params=params(),
    )(routed_slots, probs_t, back)


def fold_kernel(placement_ref, part_ref, gate_ref, up_ref, down_ref, total):
    total[...] = jnp.zeros_like(total)

    def one(slot, carry):
        expert = placement_ref[slot]
        total[expert] += part_ref[slot].astype(F32)
        return carry

    lax.fori_loop(0, part_ref.shape[0], one, 0)
    gate_ref[...] = total[:, 0].astype(BF16)
    up_ref[...] = total[:, 1].astype(BF16)
    down_ref[...] = total[:, 2].astype(BF16)


def fold(placement, parts, experts):
    slots, _, share, columns = parts.shape
    spec = pl.BlockSpec((experts, share, columns), lambda i, placement: (0, 0, 0))
    return pl.pallas_call(
        fold_kernel,
        grid_spec=pltpu.PrefetchScalarGridSpec(
            num_scalar_prefetch=1,
            grid=(1,),
            in_specs=[pl.BlockSpec((slots, 3, share, columns), lambda i, placement: (0, 0, 0, 0))],
            out_specs=[spec] * 3,
            scratch_shapes=[pltpu.VMEM((experts, 3, share, columns), F32)],
        ),
        out_shape=[jax.ShapeDtypeStruct((experts, share, columns), BF16)] * 3,
        compiler_params=params(),
    )(placement, parts)


def over_expert(value):
    return lax.all_to_all(value, "expert", split_axis=0, concat_axis=0, tiled=True)


def on_device(tokens, cotangent, routed_slots, route_probs, placement, w_gate, w_up, w_down):
    slots = lax.axis_size("expert")
    groups = lax.axis_size("dp")
    token_rows, width = tokens.shape
    columns = width // groups
    experts, share, _ = w_gate.shape

    wanted = pick(placement, w_gate, w_up, w_down, slots, columns)
    payload = pack(routed_slots.T, route_probs.T.astype(F32), tokens, cotangent, slots)
    mine = over_expert(wanted)
    mine, payload = lax.optimization_barrier((mine, payload))
    weights = lax.all_gather(mine, "dp", axis=0)
    got = over_expert(payload.reshape(slots, 2 * MAIN, -1)).reshape(payload.shape)

    parts, gate_grad, up_grad, hidden_rows, scaled = hidden_layer(got, weights)
    summed = lax.psum_scatter(parts, "dp", scatter_dimension=0)
    pairs = pair_layer(gate_grad, up_grad, hidden_rows, scaled, weights)
    back = over_expert(pairs.reshape(slots, MAIN, -1)).reshape(pairs.shape)
    token_grad, prob_grad = combine(routed_slots, route_probs.T, back, token_rows, width)

    summed, token_grad, prob_grad = lax.optimization_barrier((summed, token_grad, prob_grad))
    grads = fold(placement, over_expert(summed), experts)
    return (token_grad, prob_grad.T, *grads)


def solution(mesh):
    placed = (
        P(("dp", "expert"), None),
        P(("dp", "expert"), None),
        P(("dp", "expert"), None),
        P(("dp", "expert"), None),
        P(),
        P(None, "expert", None),
        P(None, "expert", None),
        P(None, "expert", None),
    )
    return jax.shard_map(
        on_device,
        mesh=mesh,
        in_specs=placed,
        out_specs=(
            P(("dp", "expert"), None),
            P(("dp", "expert"), None),
            P(None, "expert", "dp"),
            P(None, "expert", "dp"),
            P(None, "expert", "dp"),
        ),
        check_vma=False,
    )
```

```python
import functools

import jax
import jax.numpy as jnp
from jax import lax
from jax.experimental import pallas as pl
from jax.experimental.pallas import tpu as pltpu
from jax.sharding import PartitionSpec as P

F32 = jnp.float32
BF16 = jnp.bfloat16
I32 = jnp.int32
CAPACITY = 10
MAIN = 8
LANES = 128


def params(mib=20):
    return pltpu.CompilerParams(vmem_limit_bytes=mib * 1024 * 1024)


def far():
    return pl.BlockSpec(memory_space=pltpu.MemorySpace.HBM)


def near():
    return pl.BlockSpec(memory_space=pltpu.VMEM)


def iota(shape, dim):
    return lax.broadcasted_iota(I32, shape, dim)


def ones_where(mask):
    return jnp.where(mask, 1.0, 0.0).astype(BF16)


def matmul(a, b):
    return jnp.dot(a, b, preferred_element_type=F32)


def matmul_t(a, b):
    return lax.dot_general(a, b, (((1,), (1,)), ((), ())), preferred_element_type=F32)


def matmul_tt(a, b):
    return lax.dot_general(a, b, (((0,), (1,)), ((), ())), preferred_element_type=F32)


def pick_kernel(placement_ref, gate_ref, up_ref, down_ref, out_ref, buf, picked, sem, out_sem):
    columns = out_ref.shape[3]
    at = pl.ds(pl.multiple_of(lax.axis_index("dp") * columns, columns), columns)
    copies = [
        pltpu.make_async_copy(ref.at[:, :, at], buf.at[matrix], sem.at[matrix])
        for matrix, ref in enumerate((gate_ref, up_ref, down_ref))
    ]
    for copy in copies:
        copy.start()

    def leave(matrix):
        return pltpu.make_async_copy(picked.at[matrix], out_ref.at[:, matrix], out_sem.at[matrix])

    for matrix, copy in enumerate(copies):
        copy.wait()
        for slot in range(out_ref.shape[0]):
            picked[matrix, slot] = buf[matrix, placement_ref[slot]]
        leave(matrix).start()
    for matrix in range(3):
        leave(matrix).wait()


def pick(placement, w_gate, w_up, w_down, slots, columns):
    experts, share, _ = w_gate.shape
    return pl.pallas_call(
        pick_kernel,
        in_specs=[pl.BlockSpec(memory_space=pltpu.SMEM), far(), far(), far()],
        out_specs=far(),
        out_shape=jax.ShapeDtypeStruct((slots, 3, share, columns), BF16),
        scratch_shapes=[
            pltpu.VMEM((3, experts, share, columns), BF16),
            pltpu.VMEM((3, slots, share, columns), BF16),
            pltpu.SemaphoreType.DMA((3,)),
            pltpu.SemaphoreType.DMA((3,)),
        ],
        compiler_params=params(56),
    )(placement, w_gate, w_up, w_down)


def whole(block):
    slots, share, columns = block.shape
    return block.reshape(slots * share, columns)


def pack_kernel(slots_ref, probs_ref, tok_ref, cot_ref, out_ref):
    tokens, width = tok_ref.shape
    count = out_ref.shape[0] // (2 * MAIN)
    quarter = width // 4
    first, second = slots_ref[0:1, :], slots_ref[1:2, :]
    row = iota((count, tokens), 0)
    in_first, in_second = first == row, second == row
    before = matmul(
        ones_where(in_first | in_second),
        ones_where(iota((tokens, tokens), 0) < iota((tokens, tokens), 1)),
    )
    rank_first = jnp.sum(jnp.where(in_first, before, 0.0), axis=0, keepdims=True).astype(I32)
    rank_second = jnp.sum(jnp.where(in_second, before, 0.0), axis=0, keepdims=True).astype(I32)
    code_first = first * 16 + rank_first
    code_second = second * 16 + rank_second

    def look_up(code):
        hit_first, hit_second = code == code_first, code == code_second
        weight = jnp.sum(
            jnp.where(hit_first, probs_ref[0:1, :], 0.0) + jnp.where(hit_second, probs_ref[1:2, :], 0.0),
            axis=1,
            keepdims=True,
        )
        return hit_first | hit_second, weight

    row = iota((count * MAIN, tokens), 0)
    hit, weight = look_up((row >> 3) * 16 + (row & 7))
    chosen = ones_where(hit)
    for part in range(4):
        at = pl.ds(part * quarter, quarter)
        tok_rows = matmul(chosen, tok_ref[:, at]).reshape(count, MAIN, quarter)
        cot_rows = (weight * matmul(chosen, cot_ref[:, at])).reshape(count, MAIN, quarter)
        both = jnp.concatenate([tok_rows[:, None], cot_rows[:, None]], axis=1)
        out_ref[:, at] = both.reshape(count * 2 * MAIN, quarter).astype(BF16)

    row = iota((count * 2 * MAIN, tokens), 0)
    hit, weight = look_up((row >> 4) * 16 + MAIN + (row & 1))
    is_cot = ((row >> 1) & 1) == 1
    tok_rows = jnp.zeros((count * 2 * MAIN, quarter), F32)
    cot_rows = jnp.zeros((count * 2 * MAIN, quarter), F32)
    for part in range(4):
        here = hit & (((row >> 2) & 3) == part)
        at = pl.ds(part * quarter, quarter)
        tok_rows += matmul(ones_where(here & jnp.logical_not(is_cot)), tok_ref[:, at])
        cot_rows += matmul(ones_where(here & is_cot), cot_ref[:, at])
    out_ref[:, pl.ds(width, quarter)] = (tok_rows + weight * cot_rows).astype(BF16)


def pack(slots_t, probs_t, tokens, cotangent, slots):
    width = tokens.shape[1]
    return pl.pallas_call(
        pack_kernel,
        out_shape=jax.ShapeDtypeStruct((slots * 2 * MAIN, width + width // 4), BF16),
        compiler_params=params(),
    )(slots_t, probs_t, tokens, cotangent)


def hidden_kernel(
    got_ref, w_ref,
    part_ref, gate_grad_ref, up_grad_ref, hidden_ref, scaled_ref,
    got_buf, rest_buf, w_buf, part_buf, tok_keep, scaled_keep, gate_acc, up_acc, down_acc, both_t, hidden_t,
    grad_keep, scaled_out, got_sem, rest_sem, w_sem, part_sem, grad_sem, scaled_sem,
):
    quarters, rows, quarter = got_buf.shape
    steps, slots, _, share, columns = w_buf.shape
    units = slots * share
    each = steps // quarters
    count = rows // 16
    mains, rests = count * MAIN, count * 2
    total = mains + rests
    padded = tok_keep.shape[1]

    def got_copy(part):
        at = pl.ds(pl.multiple_of(part * quarter, quarter), quarter)
        return pltpu.make_async_copy(got_ref.at[:, at], got_buf.at[part], got_sem.at[part])

    def w_copy(part):
        at = pl.ds(part * each, each)
        return pltpu.make_async_copy(w_ref.at[at], w_buf.at[at], w_sem.at[part])

    def scaled_copy(part):
        at = pl.ds(part * each, each)
        return pltpu.make_async_copy(scaled_out.at[at], scaled_ref.at[at], scaled_sem.at[part])

    rest_copy = pltpu.make_async_copy(got_ref.at[:, pl.ds(quarters * quarter, quarter)], rest_buf, rest_sem)
    rest_copy.start()
    for part in range(2):
        got_copy(part).start()
        w_copy(part).start()
    gate_acc[...] = jnp.zeros_like(gate_acc)
    up_acc[...] = jnp.zeros_like(up_acc)
    down_acc[...] = jnp.zeros_like(down_acc)
    for step in range(steps):
        tok_keep[step, total:padded] = jnp.zeros((padded - total, columns), BF16)
        scaled_keep[step, total:padded] = jnp.zeros((padded - total, columns), BF16)
    row, column = iota((2 * rests, rows), 0), iota((2 * rests, rows), 1)
    second = jnp.where(row >= rests, 1, 0)
    inner = row - second * rests
    offset = column - (inner >> 1) * 16 - second * 2 - (inner & 1)
    rest_copy.wait()

    def forward(part, carry):
        @pl.when(part + 2 < quarters)
        def _():
            got_copy(part + 2).start()
            w_copy(part + 2).start()

        got_copy(part).wait()
        block = got_buf[part].astype(F32).reshape(count, 2, MAIN, quarter)
        rest = matmul(ones_where(offset == part * 4), rest_buf[...])
        tok = jnp.concatenate([block[:, 0].reshape(mains, quarter), rest[:rests]], axis=0).astype(BF16)
        scaled = jnp.concatenate([block[:, 1].reshape(mains, quarter), rest[rests:]], axis=0).astype(BF16)
        for i in range(each):
            at = slice(i * columns, (i + 1) * columns)
            tok_keep[part * each + i, 0:total] = tok[:, at]
            scaled_keep[part * each + i, 0:total] = scaled[:, at]
            scaled_out[part * each + i] = scaled[:, at]
        scaled_copy(part).start()
        w_copy(part).wait()
        for acc, left, matrix in ((gate_acc, tok, 0), (up_acc, tok, 1), (down_acc, scaled, 2)):
            right = jnp.concatenate([whole(w_buf[part * each + i, :, matrix]) for i in range(each)], axis=1)
            acc[...] += matmul_t(left, right)
        return carry

    lax.fori_loop(0, quarters, forward, 0)

    gate_t, up_t = both_t.at[0:units], both_t.at[units : 2 * units]
    for start in range(0, padded, 128):
        size = min(128, total - start)
        at = pl.ds(start, size)
        gate_pre, up_pre, hidden_grad = gate_acc[at, :], up_acc[at, :], down_acc[at, :]
        sigma = jax.nn.sigmoid(gate_pre)
        swish = gate_pre * sigma
        hidden = swish * up_pre
        gate_grad = hidden_grad * up_pre * sigma * (1.0 + gate_pre * (1.0 - sigma))
        up_grad = hidden_grad * swish
        for which, (value, out_t) in enumerate(((gate_grad, gate_t), (up_grad, up_t), (hidden, hidden_t))):
            grad_keep[which, at, :] = value.astype(BF16)
            if size < 128:
                value = jnp.concatenate([value, jnp.zeros((128 - size, units), F32)], axis=0)
            out_t[:, pl.ds(start, 128)] = value.T.astype(BF16)

    grad_copies = [
        pltpu.make_async_copy(grad_keep.at[which], out, grad_sem.at[which])
        for which, out in enumerate((gate_grad_ref, up_grad_ref, hidden_ref))
    ]
    for copy in grad_copies:
        copy.start()

    def part_copy(step):
        return pltpu.make_async_copy(part_buf.at[step], part_ref.at[step], part_sem.at[step])

    def backward(step):
        both = matmul(both_t[...], tok_keep[step]).reshape(2, slots, share, columns).astype(BF16)
        part_buf[step, :, 0] = both[0]
        part_buf[step, :, 1] = both[1]
        part = matmul(hidden_t[...], scaled_keep[step])
        part_buf[step, :, 2] = part.reshape(slots, share, columns).astype(BF16)
        part_copy(step).start()

    for step in range(steps):
        backward(step)
    for part in range(quarters):
        scaled_copy(part).wait()
    for copy in grad_copies:
        copy.wait()
    for step in range(steps):
        part_copy(step).wait()


def hidden_layer(got, weights):
    steps, slots, _, share, columns = weights.shape
    units = slots * share
    rows = got.shape[0]
    total = rows // 16 * CAPACITY
    padded = -(-total // 128) * 128
    quarter = steps * columns // 4
    return pl.pallas_call(
        hidden_kernel,
        in_specs=[far(), far()],
        out_specs=[far()] * 5,
        out_shape=[
            jax.ShapeDtypeStruct(weights.shape, BF16),
            jax.ShapeDtypeStruct((total, units), BF16),
            jax.ShapeDtypeStruct((total, units), BF16),
            jax.ShapeDtypeStruct((total, units), BF16),
            jax.ShapeDtypeStruct((steps, total, columns), BF16),
        ],
        scratch_shapes=[
            pltpu.VMEM((4, rows, quarter), BF16),
            pltpu.VMEM((rows, quarter), BF16),
            pltpu.VMEM(weights.shape, BF16),
            pltpu.VMEM(weights.shape, BF16),
            pltpu.VMEM((steps, padded, columns), BF16),
            pltpu.VMEM((steps, padded, columns), BF16),
            pltpu.VMEM((total, units), F32),
            pltpu.VMEM((total, units), F32),
            pltpu.VMEM((total, units), F32),
            pltpu.VMEM((2 * units, padded), BF16),
            pltpu.VMEM((units, padded), BF16),
            pltpu.VMEM((3, total, units), BF16),
            pltpu.VMEM((steps, total, columns), BF16),
            pltpu.SemaphoreType.DMA((4,)),
            pltpu.SemaphoreType.DMA,
            pltpu.SemaphoreType.DMA((4,)),
            pltpu.SemaphoreType.DMA((steps,)),
            pltpu.SemaphoreType.DMA((3,)),
            pltpu.SemaphoreType.DMA((4,)),
        ],
        compiler_params=params(56),
    )(got, weights)


def pair_kernel(
    gate_grad_ref, up_grad_ref, hidden_ref, scaled_ref, w_ref, out_ref, w_buf, rest_acc, dot_acc, w_sem
):
    steps, _, _, _, columns = w_buf.shape
    mains = out_ref.shape[0]
    count = mains // MAIN
    rests = count * 2
    width = steps * columns
    per_quarter = width // 4 // columns

    def w_copy(step):
        return pltpu.make_async_copy(w_ref.at[step], w_buf.at[step], w_sem.at[step])

    for step in range(3):
        w_copy(step).start()
    rest_acc[...] = jnp.zeros_like(rest_acc)
    dot_acc[...] = jnp.zeros_like(dot_acc)
    row, column = iota((mains, rests), 0), iota((mains, rests), 1)
    inner = row & 7
    in_place = column == (row >> 3) * 2 + (inner & 1)

    def one(step):
        if step + 3 < steps:
            w_copy(step + 3).start()
        w_copy(step).wait()
        grad = matmul(gate_grad_ref[...], whole(w_buf[step, :, 0]))
        grad += matmul(up_grad_ref[...], whole(w_buf[step, :, 1]))
        grad = grad.astype(BF16)
        out_ref[:, pl.ds(step * columns, columns)] = grad[:mains]
        placed = ones_where(in_place & ((inner >> 1) == step // per_quarter))
        rest_acc[step % per_quarter] += matmul(placed, grad[mains:])
        dot_acc[...] += matmul(hidden_ref[...], whole(w_buf[step, :, 2])) * scaled_ref[step].astype(F32)

    for step in range(steps):
        one(step)
    for which in range(per_quarter):
        out_ref[:, pl.ds(width + which * columns, columns)] = rest_acc[which].astype(BF16)
    dots = jnp.sum(dot_acc[...], axis=1, keepdims=True)
    dots = jnp.broadcast_to(dots, (mains + rests, LANES)).astype(BF16)
    moved = matmul(ones_where((inner < 2) & (column == (row >> 3) * 2 + inner)), dots[mains:])
    lane = iota((mains, LANES), 1)
    out_ref[:, pl.ds(width + width // 4, LANES)] = jnp.where(
        lane < LANES // 2, dots[:mains].astype(F32), moved
    ).astype(BF16)


def pair_layer(gate_grad, up_grad, hidden, scaled, weights):
    steps, _, _, _, columns = weights.shape
    total = gate_grad.shape[0]
    mains = total // CAPACITY * MAIN
    width = steps * columns
    return pl.pallas_call(
        pair_kernel,
        in_specs=[near(), near(), near(), near(), far()],
        out_specs=near(),
        out_shape=jax.ShapeDtypeStruct((mains, width + width // 4 + LANES), BF16),
        scratch_shapes=[
            pltpu.VMEM(weights.shape, BF16),
            pltpu.VMEM((width // 4 // columns, mains, columns), F32),
            pltpu.VMEM((total, columns), F32),
            pltpu.SemaphoreType.DMA((steps,)),
        ],
        compiler_params=params(56),
    )(gate_grad, up_grad, hidden, scaled, weights)


def combine_kernel(slots_ref, weights_ref, back_ref, token_ref, prob_ref):
    tokens, width = token_ref.shape
    mains = back_ref.shape[0]
    count = mains // MAIN
    quarter = width // 4
    first, second = slots_ref[:, 0:1], slots_ref[:, 1:2]
    column = iota((tokens, count), 1)
    in_first, in_second = first == column, second == column
    before = matmul(
        ones_where(iota((tokens, tokens), 0) > iota((tokens, tokens), 1)),
        ones_where(in_first | in_second),
    )
    rank_first = jnp.sum(jnp.where(in_first, before, 0.0), axis=1, keepdims=True).astype(I32)
    rank_second = jnp.sum(jnp.where(in_second, before, 0.0), axis=1, keepdims=True).astype(I32)
    code_first = first * 16 + rank_first
    code_second = second * 16 + rank_second

    cell = iota((tokens, mains), 1)
    code = (cell >> 3) * 16 + (cell & 7)
    main_first, main_second = code == code_first, code == code_second
    chosen = ones_where(main_first | main_second)
    code = (cell >> 3) * 16 + MAIN + (cell & 1)
    rest_hit = (code == code_first) | (code == code_second)
    rest_rows = back_ref[:, pl.ds(width, quarter)]
    for part in range(4):
        at = pl.ds(part * quarter, quarter)
        picked = ones_where(rest_hit & (((cell >> 1) & 3) == part))
        token_ref[:, at] = (matmul(chosen, back_ref[:, at]) + matmul(picked, rest_rows)).astype(BF16)

    probs = back_ref[:, pl.ds(width + quarter, LANES)]
    inner = cell & 7
    code = jnp.where(inner < 2, (cell >> 3) * 16 + MAIN + inner, -1)
    found = []
    for main_hit, mine in ((main_first, code_first), (main_second, code_second)):
        of_main = matmul_tt(probs, ones_where(main_hit))[0:1, :]
        of_rest = matmul_tt(probs, ones_where(code == mine))[LANES // 2 : LANES // 2 + 1, :]
        found.append(of_main + of_rest)
    prob_ref[...] = (jnp.concatenate(found, axis=0) / weights_ref[...].astype(F32)).astype(BF16)


def combine(routed_slots, probs_t, back, tokens, width):
    return pl.pallas_call(
        combine_kernel,
        out_shape=[
            jax.ShapeDtypeStruct((tokens, width), BF16),
            jax.ShapeDtypeStruct((2, tokens), BF16),
        ],
        compiler_params=params(),
    )(routed_slots, probs_t, back)


def fold_kernel(placement_ref, part_ref, gate_ref, up_ref, down_ref, total):
    total[...] = jnp.zeros_like(total)

    def one(slot, carry):
        expert = placement_ref[slot]
        total[expert] += part_ref[slot].astype(F32)
        return carry

    lax.fori_loop(0, part_ref.shape[0], one, 0)
    gate_ref[...] = total[:, 0].astype(BF16)
    up_ref[...] = total[:, 1].astype(BF16)
    down_ref[...] = total[:, 2].astype(BF16)


def fold(placement, parts, experts):
    slots, _, share, columns = parts.shape
    spec = pl.BlockSpec((experts, share, columns), lambda i, placement: (0, 0, 0))
    return pl.pallas_call(
        fold_kernel,
        grid_spec=pltpu.PrefetchScalarGridSpec(
            num_scalar_prefetch=1,
            grid=(1,),
            in_specs=[pl.BlockSpec((slots, 3, share, columns), lambda i, placement: (0, 0, 0, 0))],
            out_specs=[spec] * 3,
            scratch_shapes=[pltpu.VMEM((experts, 3, share, columns), F32)],
        ),
        out_shape=[jax.ShapeDtypeStruct((experts, share, columns), BF16)] * 3,
        compiler_params=params(),
    )(placement, parts)


def over_expert(value):
    return lax.all_to_all(value, "expert", split_axis=0, concat_axis=0, tiled=True)


def on_device(tokens, cotangent, routed_slots, route_probs, placement, w_gate, w_up, w_down):
    slots = lax.axis_size("expert")
    groups = lax.axis_size("dp")
    token_rows, width = tokens.shape
    columns = width // groups
    experts, share, _ = w_gate.shape

    wanted = pick(placement, w_gate, w_up, w_down, slots, columns)
    payload = pack(routed_slots.T, route_probs.T.astype(F32), tokens, cotangent, slots)
    mine = over_expert(wanted)
    mine, payload = lax.optimization_barrier((mine, payload))
    weights = lax.all_gather(mine, "dp", axis=0)
    got = over_expert(payload.reshape(slots, 2 * MAIN, -1)).reshape(payload.shape)

    parts, gate_grad, up_grad, hidden_rows, scaled = hidden_layer(got, weights)
    summed = lax.psum_scatter(parts, "dp", scatter_dimension=0)
    pairs = pair_layer(gate_grad, up_grad, hidden_rows, scaled, weights)
    back = over_expert(pairs.reshape(slots, MAIN, -1)).reshape(pairs.shape)
    token_grad, prob_grad = combine(routed_slots, route_probs.T, back, token_rows, width)

    summed, token_grad, prob_grad = lax.optimization_barrier((summed, token_grad, prob_grad))
    grads = fold(placement, over_expert(summed), experts)
    return (token_grad, prob_grad.T, *grads)


def solution(mesh):
    placed = (
        P(("dp", "expert"), None),
        P(("dp", "expert"), None),
        P(("dp", "expert"), None),
        P(("dp", "expert"), None),
        P(),
        P(None, "expert", None),
        P(None, "expert", None),
        P(None, "expert", None),
    )
    return jax.shard_map(
        on_device,
        mesh=mesh,
        in_specs=placed,
        out_specs=(
            P(("dp", "expert"), None),
            P(("dp", "expert"), None),
            P(None, "expert", "dp"),
            P(None, "expert", "dp"),
            P(None, "expert", "dp"),
        ),
        check_vma=False,
    )
```
